32 devices in a mesh: sec: 4 (over z), mpo: 8 (over y, x, core).
Axes of the slice: x: 2, y: 2, z: 4, core: 2. Of those that a mesh axis runs over, the one named last changes fastest.
Arguments:
- psi: bfloat16 [4, 512, 512], P('sec'), may hold values from -6 to 6
- left_env: bfloat16 [4, 32, 512, 512], P('sec', 'mpo'), may hold values from -0.046875 to 0.046875
- right_env: bfloat16 [4, 32, 512, 512], P('sec', 'mpo'), may hold values from -0.25 to 0.25
- dims: int32 [4, 2], P('sec'), may hold values from 1 to 16, as said below
- term_shift: int32 [32], P('mpo'), may hold values from -1 to 1, as said below
- connect: int32 [4, 32], P('sec', 'mpo'), may hold values 0 or 1
Outputs:
- h_psi: bfloat16 [4, 512, 512], P('sec', 'mpo')
The draws below stay inside these ranges and needn't reach their ends.
Inputs may be any that keep to these rules, and one draw needn't show every extreme that they name: `dims`: some sector has both sizes equal to 16. `term_shift`: some term shifts by 1 and some by -1.
All inputs are finite; a program needn't handle non-finite values. No bound on the sum of `connect` on one device may be relied on, other than what follows from the above.
Results may differ from the reference program's by a relative error of at most 0.0049.
Values may be sent and summed in bfloat16 or wider, within the bound.
No kernel may reach another device: no remote copies, remote signals or barrier semaphores. Data moves between devices by JAX's collectives and lax.ppermute only.
A program may use at most 64 MiB of HBM per device.

```python
import jax
import jax.numpy as jnp
from jax import lax

M = 512
TERMS = 32
SECTORS = 4
TILES = 16


def draw_dims(key, part):
    first_key, second_key = jax.random.split(key)
    tiles = jax.random.randint(first_key, (SECTORS, 2), 1, TILES + 1)
    chosen = jax.random.randint(second_key, (), 0, SECTORS)
    full = jnp.arange(SECTORS)[:, None] == chosen
    return jnp.where(full, TILES, tiles).astype(jnp.int32)


def draw_term_shift(key, part):
    first_key, second_key = jax.random.split(key)
    shifts = jax.random.randint(first_key, (TERMS,), -1, 2)
    order = jax.random.permutation(second_key, TERMS)
    shifts = shifts.at[order[0]].set(1).at[order[1]].set(-1)
    return shifts.astype(jnp.int32)


def place_ends(entries, own_key, low, largest):
    extent = entries.shape
    index_at = [jax.random.randint(jax.random.fold_in(own_key, axis), (), 0, extent[axis]) for axis in range(len(extent))]
    entries = entries.at[tuple(index_at)].set(low)
    longest = extent.index(max(extent))
    index_at[longest] = (index_at[longest] + 1) % extent[longest]
    return entries.at[tuple(index_at)].set(largest)


def block_levels(rng, shape, cuts, smallest, top_value):
    def one(dim, shards_of):
        heights = jax.random.uniform(jax.random.fold_in(jax.random.fold_in(rng, 6), dim), (shards_of,), jnp.float32, smallest / len(cuts), top_value / len(cuts))
        return jnp.repeat(jnp.exp(heights), shape[dim] // shards_of).reshape((-1,) + (1,) * (len(shape) - dim - 1))

    factor_of = one(*cuts[0])
    for cut in cuts[1:]:
        factor_of = factor_of * one(*cut)
    return factor_of


def gaussian(key, extent, spread, most, shards=(), kind=jnp.bfloat16):
    result = jax.random.normal(key, extent, jnp.float32) * spread
    if len(shards) > 0:
        result = block_levels(key, extent, shards, -0.22, 0.18) * result
    return jnp.clip(result, min=-most, max=most).astype(kind)


def setup_inputs(seed: int = 0) -> dict:
    key_list = jax.random.split(jax.random.key(seed), 7)
    return {
        "psi": gaussian(key_list[0], (SECTORS, M, M), 1.0, 6.0, ((0, 4),)),
        "left_env": gaussian(key_list[1], (SECTORS, TERMS, M, M), (M * TERMS) ** -0.5, 0.046875, ((0, 4), (1, 8))),
        "right_env": gaussian(key_list[2], (SECTORS, TERMS, M, M), M ** -0.5, 0.25, ((0, 4), (1, 8))),
        "dims": draw_dims(jax.random.fold_in(key_list[6], 71), 0),
        "term_shift": draw_term_shift(jax.random.fold_in(key_list[6], 71), 0),
        "connect": place_ends((jax.random.randint(key_list[5], (SECTORS, TERMS), 0, 4) < 3).astype(jnp.int32), jax.random.fold_in(key_list[5], 1), 0, 1),
    }


def reference(psi, left_env, right_env, dims, term_shift, connect):
    positions = jnp.arange(M)
    live = dims * 32
    row_ok = positions[None, :] < live[:, 0:1]
    col_ok = positions[None, :] < live[:, 1:2]
    keep = (row_ok[:, :, None] & col_ok[:, None, :])
    masked = psi * keep.astype(jnp.bfloat16)
    zero_block = jnp.zeros((1, M, M), jnp.bfloat16)
    padded = jnp.concatenate([zero_block, masked, zero_block], axis=0)

    def one_sector(sector):
        source_index = (sector + 1 - term_shift).astype(jnp.int32)
        blocks = padded[source_index] * connect[sector].astype(jnp.bfloat16)[:, None, None]
        first = jnp.einsum("wij,wjk->wik", left_env[sector].astype(jnp.float32), blocks.astype(jnp.float32))
        first = first.astype(jnp.bfloat16)
        total = jnp.einsum("wik,wkl->il", first.astype(jnp.float32), right_env[sector].astype(jnp.float32))
        return total * keep[sector].astype(jnp.float32)

    summed = lax.map(one_sector, jnp.arange(SECTORS, dtype=jnp.int32))
    return summed.astype(jnp.bfloat16)
```

```python
import jax
import jax.numpy as jnp
from jax import lax
from jax.experimental import pallas as pl
from jax.experimental.pallas import tpu as pltpu
from jax.sharding import PartitionSpec as P

AXES = ("sec", "mpo")


def halo_pairs(sectors, group):
    def other(sector, place):
        upper = (sector + place) % 2 == 0
        return sector + 1 if upper else sector - 1

    pairs = []
    for sector in range(sectors):
        for place in range(group):
            there = other(sector, place)
            if 0 <= there < sectors:
                pairs.append((sector * group + place, there * group + place))
            elif group % 4 == 0:
                pairs.append((sector * group + place, sector * group + (place ^ 2)))
    return pairs


def bit_pairs(sectors, group, bit_of):
    pairs = []
    for sector in range(sectors):
        for place in range(group):
            partner = place ^ (1 << bit_of(place % 2))
            pairs.append((sector * group + place, sector * group + partner))
    return pairs


def compute_kernel(pick_ref, live_ref, sources_ref, left_ref, right_ref, out_ref, total):
    terms = left_ref.shape[0]
    total[...] = jnp.zeros_like(total)
    for term in range(terms):

        @pl.when(pick_ref[term] < 3)
        def _():
            source = sources_ref[pick_ref[term]]
            first = jnp.dot(left_ref[term], source, preferred_element_type=jnp.float32)
            total[...] += jnp.dot(
                first.astype(jnp.bfloat16), right_ref[term], preferred_element_type=jnp.float32
            )

    rows = lax.broadcasted_iota(jnp.int32, total.shape, 0)
    cols = lax.broadcasted_iota(jnp.int32, total.shape, 1)
    keep = (rows < live_ref[0]) & (cols < live_ref[1])
    out_ref[...] = jnp.where(keep, total[...], 0.0)


def compute(pick, live, sources, left, right):
    order = left.shape[1]
    whole = pl.BlockSpec(memory_space=pltpu.VMEM)
    scalar = pl.BlockSpec(memory_space=pltpu.SMEM)
    return pl.pallas_call(
        compute_kernel,
        in_specs=[scalar, scalar, whole, whole, whole],
        out_specs=whole,
        out_shape=jax.ShapeDtypeStruct((order, order), jnp.float32),
        scratch_shapes=[pltpu.VMEM((order, order), jnp.float32)],
        compiler_params=pltpu.CompilerParams(vmem_limit_bytes=32 * 1024 * 1024),
    )(pick, live, sources, left, right)


def local(psi, left_env, right_env, dims, term_shift, connect):
    sectors, group = lax.axis_size("sec"), lax.axis_size("mpo")
    sector, place = lax.axis_index("sec"), lax.axis_index("mpo")
    core = place % 2
    order = psi.shape[1]
    bits = group.bit_length() - 1

    positions = jnp.arange(order)
    live = dims[0] * 32
    keep = (positions[:, None] < live[0]) & (positions[None, :] < live[1])
    masked = psi[0] * keep.astype(jnp.bfloat16)

    got = lax.ppermute(masked, AXES, halo_pairs(sectors, group))
    swapped = lax.ppermute(got, AXES, bit_pairs(sectors, group, lambda c: 0))
    got_upper = (sector + place) % 2 == 0
    sources = jnp.stack([masked, got, swapped])
    where_below = jnp.where(got_upper, 2, 1)
    from_sector = sector - term_shift
    pick = jnp.where(term_shift == 0, 0, jnp.where(term_shift == 1, where_below, 3 - where_below))
    used = (connect[0] != 0) & (from_sector >= 0) & (from_sector < sectors)
    pick = jnp.where(used, pick, 3).astype(jnp.int32)

    total = compute(pick, live, sources, left_env[0], right_env[0])

    blocks = total.reshape((2,) * bits + (order // group, order))
    rest = list(range(1, bits))
    orders = [rest, rest[1:] + rest[:1]]

    def halves(value, side):
        kept = lax.dynamic_index_in_dim(value, side, 0, keepdims=False)
        sent = lax.dynamic_index_in_dim(value, 1 - side, 0, keepdims=False)
        return kept, sent.astype(jnp.bfloat16)

    kept, sent = halves(jnp.moveaxis(blocks, bits - 1, 0), core)
    came = lax.ppermute(sent, AXES, bit_pairs(sectors, group, lambda c: 0))
    summed = kept + came.astype(jnp.float32)
    arranged = [jnp.transpose(summed, [bits - 1 - b for b in o] + [bits - 1, bits]) for o in orders]
    summed = jnp.where(core == 0, arranged[0], arranged[1])
    for step_at in range(bits - 1):
        bit = jnp.where(core == 0, orders[0][step_at], orders[1][step_at])
        kept, sent = halves(summed, (place >> bit) & 1)
        came = lax.ppermute(
            sent, AXES, bit_pairs(sectors, group, lambda c, step_at=step_at: orders[c][step_at])
        )
        summed = kept + came.astype(jnp.float32)
    return summed.astype(jnp.bfloat16)[None]


def solution(mesh):
    placed = (
        P("sec", None, None),
        P("sec", "mpo", None, None),
        P("sec", "mpo", None, None),
        P("sec", None),
        P("mpo"),
        P("sec", "mpo"),
    )
    return jax.shard_map(
        local, mesh=mesh, in_specs=placed, out_specs=P("sec", "mpo", None), check_vma=False
    )
```

```python
import functools

import jax
import jax.numpy as jnp
from jax import lax
from jax.experimental import pallas as pl
from jax.experimental.pallas import tpu as pltpu
from jax.sharding import PartitionSpec as P

AXES = ("sec", "mpo")
CUTS = (256, 256)
VMEM = pl.BlockSpec(memory_space=pltpu.VMEM)
HBM = pl.BlockSpec(memory_space=pltpu.HBM)
PARAMS = pltpu.CompilerParams(vmem_limit_bytes=8 * 1024 * 1024)


def halo_pairs(sectors, group):
    pairs = []
    for sector in range(sectors):
        for place in range(group):
            there = sector + 1 if (sector + place) % 2 == 0 else sector - 1
            if 0 <= there < sectors:
                pairs.append((sector * group + place, there * group + place))
            elif group % 4 == 0:
                pairs.append((sector * group + place, sector * group + (place ^ 2)))
    return pairs


def group_pairs(sectors, group, flip_of):
    return [
        (sector * group + place, sector * group + (place ^ flip_of(place % 2)))
        for sector in range(sectors)
        for place in range(group)
    ]


def in_hbm(array):
    return pltpu.with_memory_space_constraint(array, pltpu.HBM)


def dot(a, b):
    return jnp.dot(a, b, preferred_element_type=jnp.float32)


def mask_kernel(dims_hbm, psi_hbm, *refs):
    *out_refs, dims_ref, psi_ref, sems = refs
    copies = [
        pltpu.make_async_copy(dims_hbm, dims_ref, sems.at[0]),
        pltpu.make_async_copy(psi_hbm.at[0], psi_ref, sems.at[1]),
    ]
    for copy in copies:
        copy.start()
    for copy in copies:
        copy.wait()
    start = 0
    for out_ref in out_refs:
        shape = out_ref.shape
        rows = lax.broadcasted_iota(jnp.int32, shape, 0)
        cols = lax.broadcasted_iota(jnp.int32, shape, 1) + start
        keep = (rows < dims_ref[0, 0] * 32) & (cols < dims_ref[0, 1] * 32)
        piece = psi_ref[:, start : start + shape[1]]
        out_ref[...] = jnp.where(keep, piece, jnp.zeros_like(piece))
        start += shape[1]


def mask(dims, psi):
    order = psi.shape[1]
    return pl.pallas_call(
        mask_kernel,
        in_specs=[HBM, HBM],
        out_specs=[VMEM] * len(CUTS),
        out_shape=[jax.ShapeDtypeStruct((order, cut), jnp.bfloat16) for cut in CUTS],
        scratch_shapes=[
            pltpu.SMEM(dims.shape, jnp.int32),
            pltpu.VMEM(psi.shape[1:], psi.dtype),
            pltpu.SemaphoreType.DMA((2,)),
        ],
        compiler_params=PARAMS,
    )(in_hbm(dims), in_hbm(psi))


def own_kernel(sectors, shift_hbm, connect_hbm, *refs):
    *pieces, left_hbm, right_hbm, total_ref, left_ref, right_ref, code_ref, shift_ref, connect_ref, sems = refs
    terms = left_ref.shape[0]
    scalars = [
        pltpu.make_async_copy(shift_hbm, shift_ref, sems.at[2 * terms]),
        pltpu.make_async_copy(connect_hbm, connect_ref, sems.at[2 * terms + 1]),
    ]
    loads = []
    for copy in scalars:
        copy.start()
    for term in range(terms):
        pair = [
            pltpu.make_async_copy(left_hbm.at[0, term], left_ref.at[term], sems.at[2 * term]),
            pltpu.make_async_copy(right_hbm.at[0, term], right_ref.at[term], sems.at[2 * term + 1]),
        ]
        for copy in pair:
            copy.start()
        loads.append(pair)
    total_ref[...] = jnp.zeros_like(total_ref)
    for copy in scalars:
        copy.wait()

    sector, place = lax.axis_index("sec"), lax.axis_index("mpo")
    above = (sector + place) % 2 == 0
    code = jnp.int32(0)
    for term in range(terms):
        shift = shift_ref[term]
        there = sector - shift
        used = (shift != 0) & (connect_ref[0, term] != 0) & (there >= 0) & (there < sectors)
        direct = (shift < 0) == above
        code += jnp.where(used, jnp.where(direct, 2, 1), 0) << (2 * term)
    code_ref[...] = jnp.full(code_ref.shape, code, jnp.int32)

    for term in range(terms):
        for copy in loads[term]:
            copy.wait()

    @pl.loop(0, terms)
    def _(term):
        @pl.when((shift_ref[term] == 0) & (connect_ref[0, term] != 0))
        def _():
            start = 0
            for piece in pieces:
                first = dot(left_ref[term], piece[...]).astype(jnp.bfloat16)
                total_ref[...] += dot(first, right_ref[term, pl.ds(start, piece.shape[1])])
                start += piece.shape[1]


def own(sectors, term_shift, connect, pieces, left, right):
    _, terms, order, _ = left.shape
    return pl.pallas_call(
        functools.partial(own_kernel, sectors),
        in_specs=[HBM, HBM] + [VMEM] * len(pieces) + [HBM, HBM],
        out_specs=[VMEM] * 4,
        out_shape=[
            jax.ShapeDtypeStruct((order, order), jnp.float32),
            jax.ShapeDtypeStruct(left.shape[1:], left.dtype),
            jax.ShapeDtypeStruct(right.shape[1:], right.dtype),
            jax.ShapeDtypeStruct((8, 128), jnp.int32),
        ],
        scratch_shapes=[
            pltpu.SMEM(term_shift.shape, jnp.int32),
            pltpu.SMEM(connect.shape, jnp.int32),
            pltpu.SemaphoreType.DMA((2 * terms + 2,)),
        ],
        compiler_params=PARAMS,
        cost_estimate=pl.CostEstimate(flops=4 * terms * order**3, bytes_accessed=4 * terms * order**2, transcendentals=0),
    )(in_hbm(term_shift), in_hbm(connect), *pieces, in_hbm(left), in_hbm(right))


def add_terms(start, code_ref, sources, left_ref, right_ref, total_ref):
    code = code_ref[0, 0]

    @pl.loop(0, left_ref.shape[0])
    def _(term):
        choice = (code >> (2 * term)) & 3
        for which, source_ref in sources:

            @pl.when(choice == which)
            def _():
                width = source_ref.shape[1]
                first = dot(left_ref[term], source_ref[...]).astype(jnp.bfloat16)
                total_ref[...] += dot(first, right_ref[term, pl.ds(start, width)])


def shifted_kernel(start, code_ref, got_ref, swapped_ref, left_ref, right_ref, before_ref, total_ref):
    total_ref[...] = before_ref[...]
    add_terms(start, code_ref, ((2, got_ref), (1, swapped_ref)), left_ref, right_ref, total_ref)


def shifted(start, code, got, swapped, left, right, total):
    return pl.pallas_call(
        functools.partial(shifted_kernel, start),
        in_specs=[VMEM] * 6,
        out_specs=VMEM,
        out_shape=jax.ShapeDtypeStruct(total.shape, total.dtype),
        compiler_params=PARAMS,
    )(code, got, swapped, left, right, total)


def last_kernel(start, dims_hbm, code_ref, got_ref, swapped_ref, left_ref, right_ref, before_ref, kept_ref, sent_ref, total_ref, dims_ref, sem):
    copy = pltpu.make_async_copy(dims_hbm, dims_ref, sem)
    copy.start()
    total_ref[...] = before_ref[...]
    add_terms(start, code_ref, ((2, got_ref), (1, swapped_ref)), left_ref, right_ref, total_ref)
    copy.wait()
    order = total_ref.shape[0]
    blocks, height, _ = kept_ref.shape
    core = lax.axis_index("mpo") % 2
    for out_ref, side in ((sent_ref, 1 - core), (kept_ref, core)):
        for block in range(blocks):
            first = pl.multiple_of((2 * block + side) * height, height)
            rows = lax.broadcasted_iota(jnp.int32, (height, order), 0) + first
            cols = lax.broadcasted_iota(jnp.int32, (height, order), 1)
            keep = (rows < dims_ref[0, 0] * 32) & (cols < dims_ref[0, 1] * 32)
            out_ref[block] = jnp.where(keep, total_ref[pl.ds(first, height), :], 0.0).astype(out_ref.dtype)


def last(start, group, dims, code, got, swapped, left, right, total):
    order = total.shape[0]
    half = (group // 2, order // group, order)
    return pl.pallas_call(
        functools.partial(last_kernel, start),
        in_specs=[HBM] + [VMEM] * 6,
        out_specs=[VMEM, VMEM],
        out_shape=[jax.ShapeDtypeStruct(half, jnp.float32), jax.ShapeDtypeStruct(half, jnp.bfloat16)],
        scratch_shapes=[
            pltpu.VMEM((order, order), jnp.float32),
            pltpu.SMEM(dims.shape, jnp.int32),
            pltpu.SemaphoreType.DMA,
        ],
        compiler_params=PARAMS,
    )(in_hbm(dims), code, got, swapped, left, right, total)


def local(psi, left_env, right_env, dims, term_shift, connect):
    sectors, group = lax.axis_size("sec"), lax.axis_size("mpo")
    place = lax.axis_index("mpo")

    pieces = mask(dims, psi)
    to_core = group_pairs(sectors, group, lambda core: 1)
    got = [lax.ppermute(piece, AXES, halo_pairs(sectors, group)) for piece in pieces]
    total, left, right, code = own(sectors, term_shift, connect, pieces, left_env, right_env)
    got[0], total = lax.optimization_barrier((got[0], total))
    swapped = [lax.ppermute(piece, AXES, to_core) for piece in got]
    start = 0
    for at in range(len(CUTS) - 1):
        total = shifted(start, code, got[at], swapped[at], left, right, total)
        start += CUTS[at]
    kept, sent = last(start, group, dims, code, got[-1], swapped[-1], left, right, total)

    came = lax.ppermute(sent, AXES, to_core)
    value = kept + came.astype(jnp.float32)
    bits = (group // 2).bit_length() - 1
    while bits:
        taken = min(bits, 2)
        bits -= taken
        value = value.reshape((1 << taken, 1 << bits) + value.shape[1:])
        digit = (place >> (1 + bits)) & ((1 << taken) - 1)
        flips = [(1, 2, 3), (2, 1, 3)] if taken == 2 else [(1,), (1,)]
        arrived = []
        for even, odd in zip(*flips):
            flip = jnp.where(place % 2 == 0, even, odd)
            sent = lax.dynamic_index_in_dim(value, digit ^ flip, 0, keepdims=False).astype(jnp.bfloat16)
            partners = group_pairs(sectors, group, lambda core: (odd if core else even) << (1 + bits))
            arrived.append(lax.ppermute(sent, AXES, partners))
        value = lax.dynamic_index_in_dim(value, digit, 0, keepdims=False)
        for part in arrived:
            value = value + part.astype(jnp.float32)
    return value.astype(jnp.bfloat16)


def solution(mesh):
    placed = (
        P("sec", None, None),
        P("sec", "mpo", None, None),
        P("sec", "mpo", None, None),
        P("sec", None),
        P("mpo"),
        P("sec", "mpo"),
    )
    return jax.shard_map(
        local, mesh=mesh, in_specs=placed, out_specs=P("sec", "mpo", None), check_vma=False
    )
```

```python
import functools

import jax
import jax.numpy as jnp
from jax import lax
from jax.experimental import pallas as pl
from jax.experimental.pallas import tpu as pltpu
from jax.sharding import PartitionSpec as P

AXES = ("sec", "mpo")
CUTS = (256, 256)
VMEM = pl.BlockSpec(memory_space=pltpu.VMEM)
HBM = pl.BlockSpec(memory_space=pltpu.HBM)
PARAMS = pltpu.CompilerParams(vmem_limit_bytes=8 * 1024 * 1024)


def halo_pairs(sectors, group):
    pairs = []
    for sector in range(sectors):
        for place in range(group):
            there = sector + 1 if (sector + place) % 2 == 0 else sector - 1
            if 0 <= there < sectors:
                pairs.append((sector * group + place, there * group + place))
            elif group % 4 == 0:
                pairs.append((sector * group + place, sector * group + (place ^ 2)))
    return pairs


def group_pairs(sectors, group, flip_of):
    return [
        (sector * group + place, sector * group + (place ^ flip_of(place % 2)))
        for sector in range(sectors)
        for place in range(group)
    ]


def in_hbm(array):
    return pltpu.with_memory_space_constraint(array, pltpu.HBM)


def dot(a, b):
    return jnp.dot(a, b, preferred_element_type=jnp.float32)


def mask_kernel(dims_hbm, psi_hbm, *refs):
    *out_refs, dims_ref, psi_ref, sems = refs
    copies = [
        pltpu.make_async_copy(dims_hbm, dims_ref, sems.at[0]),
        pltpu.make_async_copy(psi_hbm.at[0], psi_ref, sems.at[1]),
    ]
    for copy in copies:
        copy.start()
    for copy in copies:
        copy.wait()
    start = 0
    for out_ref in out_refs:
        shape = out_ref.shape
        rows = lax.broadcasted_iota(jnp.int32, shape, 0)
        cols = lax.broadcasted_iota(jnp.int32, shape, 1) + start
        keep = (rows < dims_ref[0, 0] * 32) & (cols < dims_ref[0, 1] * 32)
        piece = psi_ref[:, start : start + shape[1]]
        out_ref[...] = jnp.where(keep, piece, jnp.zeros_like(piece))
        start += shape[1]


def mask(dims, psi):
    order = psi.shape[1]
    return pl.pallas_call(
        mask_kernel,
        in_specs=[HBM, HBM],
        out_specs=[VMEM] * len(CUTS),
        out_shape=[jax.ShapeDtypeStruct((order, cut), jnp.bfloat16) for cut in CUTS],
        scratch_shapes=[
            pltpu.SMEM(dims.shape, jnp.int32),
            pltpu.VMEM(psi.shape[1:], psi.dtype),
            pltpu.SemaphoreType.DMA((2,)),
        ],
        compiler_params=PARAMS,
    )(in_hbm(dims), in_hbm(psi))


def load_kernel(sectors, dims_hbm, shift_hbm, connect_hbm, left_hbm, right_hbm, left_ref, right_ref, code_ref, keep_ref, dims_ref, shift_ref, connect_ref, sems):
    terms = left_ref.shape[0]
    scalars = [(dims_hbm, dims_ref), (shift_hbm, shift_ref), (connect_hbm, connect_ref)]
    copies = [pltpu.make_async_copy(a, b, sems.at[at]) for at, (a, b) in enumerate(scalars)]
    for term in range(terms):
        for which, (a, b) in enumerate(((left_hbm, left_ref), (right_hbm, right_ref))):
            copies.append(pltpu.make_async_copy(a.at[0, term], b.at[term], sems.at[len(copies)]))
    for copy in copies:
        copy.start()
    for copy in copies[:3]:
        copy.wait()

    sector, place = lax.axis_index("sec"), lax.axis_index("mpo")
    above = (sector + place) % 2 == 0
    code = jnp.int32(0)
    for term in range(terms):
        shift = shift_ref[term]
        there = sector - shift
        used = (connect_ref[0, term] != 0) & (there >= 0) & (there < sectors)
        direct = (shift < 0) == above
        choice = jnp.where(shift == 0, 3, jnp.where(direct, 2, 1))
        code += jnp.where(used, choice, 0) << (2 * term)
    code_ref[...] = jnp.full(code_ref.shape, code, jnp.int32)

    rows = lax.broadcasted_iota(jnp.int32, keep_ref.shape, 0) + place * keep_ref.shape[0]
    cols = lax.broadcasted_iota(jnp.int32, keep_ref.shape, 1)
    keep = (rows < dims_ref[0, 0] * 32) & (cols < dims_ref[0, 1] * 32)
    keep_ref[...] = jnp.where(keep, 1.0, 0.0)
    for copy in copies[3:]:
        copy.wait()


def load(sectors, group, dims, term_shift, connect, left, right):
    _, terms, order, _ = left.shape
    return pl.pallas_call(
        functools.partial(load_kernel, sectors),
        in_specs=[HBM] * 5,
        out_specs=[VMEM] * 4,
        out_shape=[
            pltpu.VMEM(left.shape[1:], left.dtype),
            pltpu.VMEM(right.shape[1:], right.dtype),
            pltpu.VMEM((8, 128), jnp.int32),
            pltpu.VMEM((order // group, order), jnp.float32),
        ],
        scratch_shapes=[
            pltpu.SMEM(dims.shape, jnp.int32),
            pltpu.SMEM(term_shift.shape, jnp.int32),
            pltpu.SMEM(connect.shape, jnp.int32),
            pltpu.SemaphoreType.DMA((2 * terms + 3,)),
        ],
        compiler_params=PARAMS,
        cost_estimate=pl.CostEstimate(flops=4 * terms * order**3, bytes_accessed=4 * terms * order**2, transcendentals=0),
    )(*[in_hbm(array) for array in (dims, term_shift, connect, left, right)])


def products(start, rows_of, code_ref, own_ref, got_ref, swapped_ref, left_ref, right_ref, first_ref):
    code = code_ref[0, 0]
    terms, order, _ = right_ref.shape
    width = own_ref.shape[1]
    for term in range(terms):
        choice = (code >> (2 * term)) & 3
        own, got, swapped = own_ref[...], got_ref[...], swapped_ref[...]
        source = jnp.where(choice == 3, own, jnp.where(choice == 2, got, jnp.where(choice == 1, swapped, jnp.zeros_like(own))))
        first_ref[:, term * width : (term + 1) * width] = dot(rows_of(left_ref, term), source).astype(jnp.bfloat16)
    right = right_ref[:, start : start + width, :].reshape(terms * width, order)
    return dot(first_ref[...], right)


def part_kernel(start, code_ref, own_ref, got_ref, swapped_ref, left_ref, right_ref, *refs):
    *before, total_ref, first_ref = refs
    total = products(start, lambda left, term: left[term], code_ref, own_ref, got_ref, swapped_ref, left_ref, right_ref, first_ref)
    for ref in before:
        total += ref[...]
    total_ref[...] = total


def part(start, code, own, got, swapped, left, right, before):
    terms, order, _ = left.shape
    operands = [code, own, got, swapped, left, right, *before]
    return pl.pallas_call(
        functools.partial(part_kernel, start),
        in_specs=[VMEM] * len(operands),
        out_specs=VMEM,
        out_shape=pltpu.VMEM((order, order), jnp.float32),
        scratch_shapes=[pltpu.VMEM((order, terms * own.shape[1]), jnp.bfloat16)],
        compiler_params=PARAMS,
    )(*operands)


def half_kernel(start, theirs, code_ref, own_ref, got_ref, swapped_ref, left_ref, right_ref, before_ref, out_ref, first_ref):
    blocks, height, _ = out_ref.shape
    core = lax.axis_index("mpo") % 2
    side = 1 - core if theirs else core
    places = [pl.ds(pl.multiple_of((2 * block + side) * height, height), height) for block in range(blocks)]

    def rows_of(left, term):
        return jnp.concatenate([left[term, at] for at in places], axis=0)

    total = products(start, rows_of, code_ref, own_ref, got_ref, swapped_ref, left_ref, right_ref, first_ref)
    for block, at in enumerate(places):
        value = total[block * height : (block + 1) * height] + before_ref[at]
        out_ref[block] = value.astype(out_ref.dtype)


def half(start, theirs, group, code, own, got, swapped, left, right, before):
    terms, order, _ = left.shape
    return pl.pallas_call(
        functools.partial(half_kernel, start, theirs),
        in_specs=[VMEM] * 7,
        out_specs=VMEM,
        out_shape=pltpu.VMEM((group // 2, order // group, order), jnp.bfloat16 if theirs else jnp.float32),
        scratch_shapes=[pltpu.VMEM((order // 2, terms * own.shape[1]), jnp.bfloat16)],
        compiler_params=PARAMS,
        cost_estimate=pl.CostEstimate(flops=2 * terms * order**2 * own.shape[1], bytes_accessed=0, transcendentals=0),
    )(code, own, got, swapped, left, right, before)


def split_kernel(shift, flips, *refs):
    ways = 1 + len(flips[0])
    *addends, own_ref = refs[: len(refs) - ways + 1]
    send_refs = refs[len(refs) - ways + 1 :]
    count = own_ref.shape[0]
    place = lax.axis_index("mpo")
    digit = (place >> shift) & (ways - 1)

    def summed(block):
        value = addends[0][block]
        for other in addends[1:]:
            value += other[block].astype(jnp.float32)
        return value

    for ref, even, odd in zip(send_refs, *flips):
        flip = jnp.where(place % 2 == 0, even, odd)
        for at in range(count):
            ref[at] = summed((digit ^ flip) * count + at).astype(ref.dtype)
    for at in range(count):
        own_ref[at] = summed(digit * count + at)


def split(addends, shift, flips):
    ways = 1 + len(flips[0])
    blocks, height, width = addends[0].shape
    shape = (blocks // ways, height, width)
    own, *sends = pl.pallas_call(
        functools.partial(split_kernel, shift, flips),
        in_specs=[VMEM] * len(addends),
        out_specs=[VMEM] * ways,
        out_shape=[pltpu.VMEM(shape, jnp.float32)] + [pltpu.VMEM(shape, jnp.bfloat16)] * (ways - 1),
        compiler_params=PARAMS,
    )(*addends)
    return sends, own


def local(psi, left_env, right_env, dims, term_shift, connect):
    sectors, group = lax.axis_size("sec"), lax.axis_size("mpo")
    place = lax.axis_index("mpo")
    order = psi.shape[1]

    pieces = mask(dims, psi)
    to_core = group_pairs(sectors, group, lambda core: 1)
    got = [lax.ppermute(piece, AXES, halo_pairs(sectors, group)) for piece in pieces]
    left, right, code, keep = load(sectors, group, dims, term_shift, connect, left_env, right_env)
    got[0], code = lax.optimization_barrier((got[0], code))
    swapped = [lax.ppermute(piece, AXES, to_core) for piece in got]
    start, total = 0, []
    for at in range(len(CUTS) - 1):
        total = [part(start, code, pieces[at], got[at], swapped[at], left, right, total)]
        start += CUTS[at]
    last = (code, pieces[-1], got[-1], swapped[-1], left, right)
    if (order // group) % 16 == 0:
        sent = half(start, True, group, *last, *total)
        kept = half(start, False, group, *last, *total)
    else:
        blocks = part(start, *last, total).reshape(group // 2, 2, order // group, order)
        kept = lax.dynamic_index_in_dim(blocks, place % 2, 1, keepdims=False)
        sent = lax.dynamic_index_in_dim(blocks, 1 - place % 2, 1, keepdims=False).astype(jnp.bfloat16)

    addends = [kept, lax.ppermute(sent, AXES, to_core)]
    bits = (group // 2).bit_length() - 1
    while bits:
        taken = min(bits, 2)
        bits -= taken
        flips = [(1, 2, 3), (2, 1, 3)] if taken == 2 else [(1,), (1,)]
        sends, own = split(addends, 1 + bits, flips)
        addends = [own]
        for sent, even, odd in zip(sends, *flips):
            partners = group_pairs(sectors, group, lambda core: (odd if core else even) << (1 + bits))
            addends.append(lax.ppermute(sent, AXES, partners))
    value = addends[0]
    for other in addends[1:]:
        value = value + other.astype(jnp.float32)
    value = jnp.where(keep != 0, value.reshape(keep.shape), 0.0)
    return value.astype(jnp.bfloat16)[None]


def solution(mesh):
    placed = (
        P("sec", None, None),
        P("sec", "mpo", None, None),
        P("sec", "mpo", None, None),
        P("sec", None),
        P("mpo"),
        P("sec", "mpo"),
    )
    return jax.shard_map(
        local, mesh=mesh, in_specs=placed, out_specs=P("sec", "mpo", None), check_vma=False
    )
```

```python
import functools

import jax
import jax.numpy as jnp
from jax import lax
from jax.experimental import pallas as pl
from jax.experimental.pallas import tpu as pltpu
from jax.sharding import PartitionSpec as P

AXES = ("sec", "mpo")
CUTS = (256, 256)
FLIPS = {4: (3, 1, 2), 2: (1,)}
VMEM = pl.BlockSpec(memory_space=pltpu.VMEM)
HBM = pl.BlockSpec(memory_space=pltpu.HBM)
PARAMS = pltpu.CompilerParams(vmem_limit_bytes=8 * 1024 * 1024)


def halo_pairs(sectors, group):
    pairs = []
    for sector in range(sectors):
        for place in range(group):
            there = sector + 1 if place % 2 == 0 else sector - 1
            if 0 <= there < sectors:
                pairs.append((sector * group + place, there * group + (place ^ 1)))
            elif group % 4 == 0:
                pairs.append((sector * group + place, sector * group + (place ^ 2)))
    return pairs


def group_pairs(sectors, group, flip):
    return [
        (sector * group + place, sector * group + (place ^ flip))
        for sector in range(sectors)
        for place in range(group)
    ]


def stages_of(group):
    bits, stages = (group // 2).bit_length() - 1, []
    while bits:
        taken = min(bits, 2)
        bits -= taken
        stages.append((bits, 1 << taken))
    return stages


def core_for(group, place, chip):
    core, differ = place % 2, (place // 2) ^ chip
    for bit, ways in stages_of(group):
        core = core ^ jnp.where((differ >> bit) & (ways - 1) != 0, 1, 0)
    return core


def in_hbm(array):
    return pltpu.with_memory_space_constraint(array, pltpu.HBM)


def dot(a, b):
    return jnp.dot(a, b, preferred_element_type=jnp.float32)


def mask_kernel(dims_hbm, psi_hbm, *refs):
    *out_refs, dims_ref, psi_ref, sems = refs
    copies = [
        pltpu.make_async_copy(dims_hbm, dims_ref, sems.at[0]),
        pltpu.make_async_copy(psi_hbm.at[0], psi_ref, sems.at[1]),
    ]
    for copy in copies:
        copy.start()
    for copy in copies:
        copy.wait()
    start = 0
    for out_ref in out_refs:
        shape = out_ref.shape
        rows = lax.broadcasted_iota(jnp.int32, shape, 0)
        cols = lax.broadcasted_iota(jnp.int32, shape, 1) + start
        keep = (rows < dims_ref[0, 0] * 32) & (cols < dims_ref[0, 1] * 32)
        piece = psi_ref[:, start : start + shape[1]]
        out_ref[...] = jnp.where(keep, piece, jnp.zeros_like(piece))
        start += shape[1]


def mask(dims, psi):
    order = psi.shape[1]
    return pl.pallas_call(
        mask_kernel,
        in_specs=[HBM, HBM],
        out_specs=[VMEM] * len(CUTS),
        out_shape=[jax.ShapeDtypeStruct((order, cut), jnp.bfloat16) for cut in CUTS],
        scratch_shapes=[
            pltpu.SMEM(dims.shape, jnp.int32),
            pltpu.VMEM(psi.shape[1:], psi.dtype),
            pltpu.SemaphoreType.DMA((2,)),
        ],
        compiler_params=PARAMS,
    )(in_hbm(dims), in_hbm(psi))


def load_kernel(sectors, dims_hbm, shift_hbm, connect_hbm, left_hbm, right_hbm, left_ref, right_ref, code_ref, keep_ref, dims_ref, shift_ref, connect_ref, sems):
    terms = left_ref.shape[0]
    scalars = [(dims_hbm, dims_ref), (shift_hbm, shift_ref), (connect_hbm, connect_ref)]
    copies = [pltpu.make_async_copy(a, b, sems.at[at]) for at, (a, b) in enumerate(scalars)]
    for term in range(terms):
        for which, (a, b) in enumerate(((left_hbm, left_ref), (right_hbm, right_ref))):
            copies.append(pltpu.make_async_copy(a.at[0, term], b.at[term], sems.at[len(copies)]))
    for copy in copies:
        copy.start()
    for copy in copies[:3]:
        copy.wait()

    sector, place = lax.axis_index("sec"), lax.axis_index("mpo")
    above = place % 2 == 0
    code = jnp.int32(0)
    for term in range(terms):
        shift = shift_ref[term]
        there = sector - shift
        used = (connect_ref[0, term] != 0) & (there >= 0) & (there < sectors)
        direct = (shift < 0) == above
        choice = jnp.where(shift == 0, 3, jnp.where(direct, 2, 1))
        code += jnp.where(used, choice, 0) << (2 * term)
    code_ref[...] = jnp.full(code_ref.shape, code, jnp.int32)

    rows = lax.broadcasted_iota(jnp.int32, keep_ref.shape, 0) + place * keep_ref.shape[0]
    cols = lax.broadcasted_iota(jnp.int32, keep_ref.shape, 1)
    keep = (rows < dims_ref[0, 0] * 32) & (cols < dims_ref[0, 1] * 32)
    keep_ref[...] = jnp.where(keep, 1.0, 0.0)
    for copy in copies[3:]:
        copy.wait()


def load(sectors, group, dims, term_shift, connect, left, right):
    _, terms, order, _ = left.shape
    return pl.pallas_call(
        functools.partial(load_kernel, sectors),
        in_specs=[HBM] * 5,
        out_specs=[VMEM] * 4,
        out_shape=[
            pltpu.VMEM(left.shape[1:], left.dtype),
            pltpu.VMEM(right.shape[1:], right.dtype),
            pltpu.VMEM((8, 128), jnp.int32),
            pltpu.VMEM((order // group, order), jnp.float32),
        ],
        scratch_shapes=[
            pltpu.SMEM(dims.shape, jnp.int32),
            pltpu.SMEM(term_shift.shape, jnp.int32),
            pltpu.SMEM(connect.shape, jnp.int32),
            pltpu.SemaphoreType.DMA((2 * terms + 3,)),
        ],
        compiler_params=PARAMS,
        cost_estimate=pl.CostEstimate(flops=4 * terms * order**3, bytes_accessed=4 * terms * order**2, transcendentals=0),
    )(*[in_hbm(array) for array in (dims, term_shift, connect, left, right)])


def products(start, rows_of, code_ref, own_ref, got_ref, swapped_ref, left_ref, right_ref, first_ref):
    code = code_ref[0, 0]
    terms, order, _ = right_ref.shape
    width = own_ref.shape[1]
    for term in range(terms):
        choice = (code >> (2 * term)) & 3
        own, got, swapped = own_ref[...], got_ref[...], swapped_ref[...]
        source = jnp.where(choice == 3, own, jnp.where(choice == 2, got, jnp.where(choice == 1, swapped, jnp.zeros_like(own))))
        first_ref[:, term * width : (term + 1) * width] = dot(rows_of(left_ref, term), source).astype(jnp.bfloat16)
    right = right_ref[:, start : start + width, :].reshape(terms * width, order)
    return dot(first_ref[...], right)


def part_kernel(start, code_ref, own_ref, got_ref, swapped_ref, left_ref, right_ref, *refs):
    *before, total_ref, first_ref = refs
    total = products(start, lambda left, term: left[term], code_ref, own_ref, got_ref, swapped_ref, left_ref, right_ref, first_ref)
    for ref in before:
        total += ref[...]
    total_ref[...] = total


def part(start, code, own, got, swapped, left, right, before):
    terms, order, _ = left.shape
    operands = [code, own, got, swapped, left, right, *before]
    return pl.pallas_call(
        functools.partial(part_kernel, start),
        in_specs=[VMEM] * len(operands),
        out_specs=VMEM,
        out_shape=pltpu.VMEM((order, order), jnp.float32),
        scratch_shapes=[pltpu.VMEM((order, terms * own.shape[1]), jnp.bfloat16)],
        compiler_params=PARAMS,
    )(*operands)


def row_blocks(group, height, theirs):
    place = lax.axis_index("mpo")
    firsts = []
    for chip in range(group // 2):
        core = core_for(group, place, chip)
        firsts.append((2 * chip + (1 - core if theirs else core)) * height)
    return [pl.ds(pl.multiple_of(first, height), height) for first in firsts]


def half_kernel(start, theirs, group, code_ref, own_ref, got_ref, swapped_ref, left_ref, right_ref, before_ref, out_ref, first_ref):
    height = out_ref.shape[1]
    places = row_blocks(group, height, theirs)

    def rows_of(left, term):
        return jnp.concatenate([left[term, at] for at in places], axis=0)

    total = products(start, rows_of, code_ref, own_ref, got_ref, swapped_ref, left_ref, right_ref, first_ref)
    for block, at in enumerate(places):
        value = total[block * height : (block + 1) * height] + before_ref[at]
        out_ref[block] = value.astype(out_ref.dtype)


def half(start, theirs, group, code, own, got, swapped, left, right, before):
    terms, order, _ = left.shape
    return pl.pallas_call(
        functools.partial(half_kernel, start, theirs, group),
        in_specs=[VMEM] * 7,
        out_specs=VMEM,
        out_shape=pltpu.VMEM((group // 2, order // group, order), jnp.bfloat16 if theirs else jnp.float32),
        scratch_shapes=[pltpu.VMEM((order // 2, terms * own.shape[1]), jnp.bfloat16)],
        compiler_params=PARAMS,
        cost_estimate=pl.CostEstimate(flops=2 * terms * order**2 * own.shape[1], bytes_accessed=0, transcendentals=0),
    )(code, own, got, swapped, left, right, before)


def pick_kernel(group, total_ref, sent_ref, kept_ref):
    for out_ref, theirs in ((sent_ref, True), (kept_ref, False)):
        for block, at in enumerate(row_blocks(group, out_ref.shape[1], theirs)):
            out_ref[block] = total_ref[at].astype(out_ref.dtype)


def pick(group, total):
    order = total.shape[0]
    shape = (group // 2, order // group, order)
    return pl.pallas_call(
        functools.partial(pick_kernel, group),
        in_specs=[VMEM],
        out_specs=[VMEM, VMEM],
        out_shape=[pltpu.VMEM(shape, jnp.bfloat16), pltpu.VMEM(shape, jnp.float32)],
        compiler_params=PARAMS,
    )(total)


def split_kernel(bit, flips, *refs):
    ways = 1 + len(flips)
    *addends, own_ref = refs[: len(refs) - ways + 1]
    send_refs = refs[len(refs) - ways + 1 :]
    count = own_ref.shape[0]
    digit = (lax.axis_index("mpo") >> (1 + bit)) & (ways - 1)

    def summed(block):
        value = addends[0][block]
        for other in addends[1:]:
            value += other[block].astype(jnp.float32)
        return value

    for ref, flip in zip(send_refs, flips):
        for at in range(count):
            ref[at] = summed((digit ^ flip) * count + at).astype(ref.dtype)
    for at in range(count):
        own_ref[at] = summed(digit * count + at)


def split(addends, bit, flips):
    ways = 1 + len(flips)
    blocks, height, width = addends[0].shape
    shape = (blocks // ways, height, width)
    own, *sends = pl.pallas_call(
        functools.partial(split_kernel, bit, flips),
        in_specs=[VMEM] * len(addends),
        out_specs=[VMEM] * ways,
        out_shape=[pltpu.VMEM(shape, jnp.float32)] + [pltpu.VMEM(shape, jnp.bfloat16)] * (ways - 1),
        compiler_params=PARAMS,
    )(*addends)
    return sends, own


def local(psi, left_env, right_env, dims, term_shift, connect):
    sectors, group = lax.axis_size("sec"), lax.axis_size("mpo")
    order = psi.shape[1]

    pieces = mask(dims, psi)
    to_core = group_pairs(sectors, group, 1)
    got = [lax.ppermute(piece, AXES, halo_pairs(sectors, group)) for piece in pieces]
    left, right, code, keep = load(sectors, group, dims, term_shift, connect, left_env, right_env)
    got[0], code = lax.optimization_barrier((got[0], code))
    swapped = [lax.ppermute(piece, AXES, to_core) for piece in got]
    start, total = 0, []
    for at in range(len(CUTS) - 1):
        total = [part(start, code, pieces[at], got[at], swapped[at], left, right, total)]
        start += CUTS[at]
    last = (code, pieces[-1], got[-1], swapped[-1], left, right)
    if (order // group) % 16 == 0:
        sent = half(start, True, group, *last, *total)
        kept = half(start, False, group, *last, *total)
    else:
        sent, kept = pick(group, part(start, *last, total))

    addends = [kept, lax.ppermute(sent, AXES, to_core)]
    for bit, ways in stages_of(group):
        flips = FLIPS[ways]
        sends, own = split(addends, bit, flips)
        addends = [own]
        for sent, flip in zip(sends, flips):
            addends.append(lax.ppermute(sent, AXES, group_pairs(sectors, group, (flip << (1 + bit)) | 1)))
    value = addends[0]
    for other in addends[1:]:
        value = value + other.astype(jnp.float32)
    value = jnp.where(keep != 0, value.reshape(keep.shape), 0.0)
    return value.astype(jnp.bfloat16)[None]


def solution(mesh):
    placed = (
        P("sec", None, None),
        P("sec", "mpo", None, None),
        P("sec", "mpo", None, None),
        P("sec", None),
        P("mpo"),
        P("sec", "mpo"),
    )
    return jax.shard_map(
        local, mesh=mesh, in_specs=placed, out_specs=P("sec", "mpo", None), check_vma=False
    )
```

```python
import functools

import jax
import jax.numpy as jnp
from jax import lax
from jax.experimental import pallas as pl
from jax.experimental.pallas import tpu as pltpu
from jax.sharding import PartitionSpec as P

AXES = ("sec", "mpo")
CUTS = (256, 256)
FLIPS = {4: (3, 1, 2), 2: (1,), 1: ()}
VMEM = pl.BlockSpec(memory_space=pltpu.VMEM)
HBM = pl.BlockSpec(memory_space=pltpu.HBM)
PARAMS = pltpu.CompilerParams(vmem_limit_bytes=8 * 1024 * 1024)


def halo_pairs(sectors, group):
    pairs = []
    for sector in range(sectors):
        for place in range(group):
            there = sector + 1 if place % 2 == 0 else sector - 1
            if 0 <= there < sectors:
                pairs.append((sector * group + place, there * group + (place ^ 1)))
            elif group % 4 == 0:
                pairs.append((sector * group + place, sector * group + (place ^ 2)))
    return pairs


def group_pairs(sectors, group, flip):
    return [
        (sector * group + place, sector * group + (place ^ flip))
        for sector in range(sectors)
        for place in range(group)
    ]


def stages_of(group):
    bits, stages = (group // 2).bit_length() - 1, []
    while bits:
        taken = min(bits, 2)
        bits -= taken
        stages.append((bits, 1 << taken))
    return stages or [(0, 1)]


def parity(number):
    for shift in (8, 4, 2, 1):
        number = number ^ (number >> shift)
    return number & 1


def in_hbm(array):
    return pltpu.with_memory_space_constraint(array, pltpu.HBM)


def dot(a, b):
    return jnp.dot(a, b, preferred_element_type=jnp.float32)


def mask_kernel(start, dims_hbm, psi_hbm, out_ref, dims_ref, psi_ref, sems):
    parts = sems.shape[0] - 1
    rows, width = out_ref.shape[0] // parts, out_ref.shape[1]
    dims_copy = pltpu.make_async_copy(dims_hbm, dims_ref, sems.at[parts])
    dims_copy.start()
    copies = []
    for at in range(parts):
        from_ref = psi_hbm.at[0, pl.ds(at * rows, rows), pl.ds(start, width)]
        copies.append(pltpu.make_async_copy(from_ref, psi_ref.at[pl.ds(at * rows, rows)], sems.at[at]))
        copies[-1].start()
    dims_copy.wait()
    for at in range(parts):
        row = lax.broadcasted_iota(jnp.int32, (rows, width), 0) + at * rows
        col = lax.broadcasted_iota(jnp.int32, (rows, width), 1) + start
        keep = (row < dims_ref[0, 0] * 32) & (col < dims_ref[0, 1] * 32)
        copies[at].wait()
        piece = psi_ref[pl.ds(at * rows, rows)]
        out_ref[pl.ds(at * rows, rows)] = jnp.where(keep, piece, jnp.zeros_like(piece))


def mask(start, width, dims, psi):
    order, parts = psi.shape[1], 8
    return pl.pallas_call(
        functools.partial(mask_kernel, start),
        in_specs=[HBM, HBM],
        out_specs=VMEM,
        out_shape=pltpu.VMEM((order, width), psi.dtype),
        scratch_shapes=[
            pltpu.SMEM(dims.shape, jnp.int32),
            pltpu.VMEM((order, width), psi.dtype),
            pltpu.SemaphoreType.DMA((parts + 1,)),
        ],
        compiler_params=PARAMS,
        cost_estimate=pl.CostEstimate(flops=50000000000 if start else 0, bytes_accessed=0, transcendentals=0),
    )(in_hbm(dims), in_hbm(psi))


def load_kernel(sectors, dims_hbm, shift_hbm, connect_hbm, left_hbm, right_hbm, left_ref, right_ref, code_ref, keep_ref, dims_ref, shift_ref, connect_ref, sems):
    terms = left_ref.shape[0]
    scalars = [(dims_hbm, dims_ref), (shift_hbm, shift_ref), (connect_hbm, connect_ref)]
    copies = [pltpu.make_async_copy(a, b, sems.at[at]) for at, (a, b) in enumerate(scalars)]
    for term in range(terms):
        for which, (a, b) in enumerate(((left_hbm, left_ref), (right_hbm, right_ref))):
            copies.append(pltpu.make_async_copy(a.at[0, term], b.at[term], sems.at[len(copies)]))
    for copy in copies:
        copy.start()
    for copy in copies[:3]:
        copy.wait()

    sector, place = lax.axis_index("sec"), lax.axis_index("mpo")
    above = place % 2 == 0
    code = jnp.int32(0)
    for term in range(terms):
        shift = shift_ref[term]
        there = sector - shift
        used = (connect_ref[0, term] != 0) & (there >= 0) & (there < sectors)
        direct = (shift < 0) == above
        choice = jnp.where(shift == 0, 3, jnp.where(direct, 2, 1))
        code += jnp.where(used, choice, 0) << (2 * term)
    code_ref[...] = jnp.full(code_ref.shape, code, jnp.int32)

    rows = lax.broadcasted_iota(jnp.int32, keep_ref.shape, 0) + place * keep_ref.shape[0]
    cols = lax.broadcasted_iota(jnp.int32, keep_ref.shape, 1)
    keep = (rows < dims_ref[0, 0] * 32) & (cols < dims_ref[0, 1] * 32)
    keep_ref[...] = jnp.where(keep, 1.0, 0.0)
    for copy in copies[3:]:
        copy.wait()


def load(sectors, group, dims, term_shift, connect, left, right):
    _, terms, order, _ = left.shape
    return pl.pallas_call(
        functools.partial(load_kernel, sectors),
        in_specs=[HBM] * 5,
        out_specs=[VMEM] * 4,
        out_shape=[
            pltpu.VMEM(left.shape[1:], left.dtype),
            pltpu.VMEM(right.shape[1:], right.dtype),
            pltpu.VMEM((8, 128), jnp.int32),
            pltpu.VMEM((order // group, order), jnp.float32),
        ],
        scratch_shapes=[
            pltpu.SMEM(dims.shape, jnp.int32),
            pltpu.SMEM(term_shift.shape, jnp.int32),
            pltpu.SMEM(connect.shape, jnp.int32),
            pltpu.SemaphoreType.DMA((2 * terms + 3,)),
        ],
        compiler_params=PARAMS,
        cost_estimate=pl.CostEstimate(flops=4 * terms * order**3, bytes_accessed=4 * terms * order**2, transcendentals=0),
    )(*[in_hbm(array) for array in (dims, term_shift, connect, left, right)])


def row_blocks(group, height, flips):
    place = lax.axis_index("mpo")
    bit, ways = stages_of(group)[0]
    digit = (place >> (1 + bit)) & (ways - 1)
    firsts = []
    for flip in (0, *flips):
        for at in range(1 << bit):
            chip = ((digit ^ flip) << bit) + at
            firsts.append((2 * chip + (parity(place) ^ parity(chip))) * height)
    return [pl.ds(pl.multiple_of(first, height), height) for first in firsts]


def products(start, places, sources, groups, first_ref):
    own, got, swapped = (ref[...] for ref in sources)
    total = None
    for code_ref, left_ref, right_ref, direct in groups:
        code = code_ref[0, 0]
        terms, order, _ = right_ref.shape
        width = own.shape[1]
        for term in range(terms):
            choice = (code >> (2 * term)) & 3
            source = jnp.where(choice == direct, got, jnp.where(choice == 3 - direct, swapped, jnp.zeros_like(own)))
            source = jnp.where(choice == 3, own, source)
            left = left_ref[term] if places is None else jnp.concatenate([left_ref[term, at] for at in places], axis=0)
            first_ref[:, term * width : (term + 1) * width] = dot(left, source).astype(jnp.bfloat16)
        right = right_ref[:, start : start + width, :].reshape(terms * width, order)
        total = dot(first_ref[...], right) if total is None else total + dot(first_ref[...], right)
    return total


def sums_kernel(start, group, height, flips, last, *refs):
    sources, (code, left, right, code_2, left_2, right_2), refs = refs[:3], refs[3:9], refs[9:]
    order = left.shape[1]
    groups = ((code, left, right, 2), (code_2, left_2.at[0], right_2.at[0], 1))
    places = row_blocks(group, height, flips)
    narrow = height % 16 == 0
    *before, first_ref, total_ref = refs[: -(2 + (1 + len(flips) if last else 1))] + refs[-2:]
    outs = refs[len(before) : -2]
    total = products(start, places if narrow else None, sources, groups, first_ref)
    for ref in before:
        total += ref[...]
    if not last:
        outs[0][...] = total
        return
    if not narrow:
        total_ref[...] = total
    each = len(places) // len(outs)
    for which, out_ref in enumerate(outs):
        for at in range(each):
            block = which * each + at
            value = total[block * height : (block + 1) * height] if narrow else total_ref[places[block]]
            out_ref[at] = value.astype(out_ref.dtype)


def sums(start, group, flips, last, sources, terms, before):
    count, order, _ = terms[1].shape
    height = order // group
    rows = order // 2 if height % 16 == 0 else order
    shape = (group // 2 // (1 + len(flips)), height, order)
    if last:
        outs = [pltpu.VMEM(shape, jnp.float32)] + [pltpu.VMEM(shape, jnp.bfloat16)] * len(flips)
    else:
        outs = [pltpu.VMEM((rows, order), jnp.float32)]
    operands = [*sources, *terms, *before]
    return pl.pallas_call(
        functools.partial(sums_kernel, start, group, height, flips, last),
        in_specs=[VMEM] * len(operands),
        out_specs=[VMEM] * len(outs),
        out_shape=outs,
        scratch_shapes=[
            pltpu.VMEM((rows, count * sources[0].shape[1]), jnp.bfloat16),
            pltpu.VMEM((order, order) if height % 16 else (8, 128), jnp.float32),
        ],
        compiler_params=PARAMS,
    )(*operands)


def split_kernel(bit, flips, *refs):
    ways = 1 + len(flips)
    *addends, own_ref = refs[: len(refs) - ways + 1]
    send_refs = refs[len(refs) - ways + 1 :]
    count = own_ref.shape[0]
    digit = (lax.axis_index("mpo") >> (1 + bit)) & (ways - 1)

    def summed(block):
        value = addends[0][block]
        for other in addends[1:]:
            value += other[block].astype(jnp.float32)
        return value

    for ref, flip in zip(send_refs, flips):
        for at in range(count):
            ref[at] = summed((digit ^ flip) * count + at).astype(ref.dtype)
    for at in range(count):
        own_ref[at] = summed(digit * count + at)


def split(addends, bit, flips):
    ways = 1 + len(flips)
    blocks, height, width = addends[0].shape
    shape = (blocks // ways, height, width)
    own, *sends = pl.pallas_call(
        functools.partial(split_kernel, bit, flips),
        in_specs=[VMEM] * len(addends),
        out_specs=[VMEM] * ways,
        out_shape=[pltpu.VMEM(shape, jnp.float32)] + [pltpu.VMEM(shape, jnp.bfloat16)] * (ways - 1),
        compiler_params=PARAMS,
    )(*addends)
    return sends, own


def local(psi, left_env, right_env, dims, term_shift, connect):
    sectors, group = lax.axis_size("sec"), lax.axis_size("mpo")
    order = psi.shape[1]

    pieces, start = [], 0
    for cut in CUTS:
        pieces.append(mask(start, cut, dims, psi))
        pieces[-1], psi = lax.optimization_barrier((pieces[-1], psi))
        start += cut
    to_core = group_pairs(sectors, group, 1)
    got = [lax.ppermute(piece, AXES, halo_pairs(sectors, group)) for piece in pieces]
    left_env, right_env, pieces[0] = lax.optimization_barrier((left_env, right_env, pieces[0]))
    left_2, right_2 = (lax.ppermute(env, AXES, to_core) for env in (left_env, right_env))
    left, right, code, keep = load(sectors, group, dims, term_shift, connect, left_env, right_env)
    code_2 = lax.ppermute(code, AXES, to_core)
    got[0], code = lax.optimization_barrier((got[0], code))
    got[-1], code_2 = lax.optimization_barrier((got[-1], code_2))
    swapped = [lax.ppermute(piece, AXES, to_core) for piece in got]

    terms = (code, left, right, code_2, left_2, right_2)
    stages = stages_of(group)
    start, addends = 0, []
    for at, cut in enumerate(CUTS):
        last = at == len(CUTS) - 1
        addends = sums(start, group, FLIPS[stages[0][1]], last, (pieces[at], got[at], swapped[at]), terms, addends)
        start += cut
    own, *sends = addends
    for at, (bit, ways) in enumerate(stages):
        if at > 0:
            sends, own = split(addends, bit, FLIPS[ways])
        addends = [own]
        for sent, flip in zip(sends, FLIPS[ways]):
            addends.append(lax.ppermute(sent, AXES, group_pairs(sectors, group, (flip << (1 + bit)) | parity(flip))))
    value = addends[0]
    for other in addends[1:]:
        value = value + other.astype(jnp.float32)
    value = jnp.where(keep != 0, value.reshape(keep.shape), 0.0)
    return value.astype(jnp.bfloat16)[None]


def solution(mesh):
    placed = (
        P("sec", None, None),
        P("sec", "mpo", None, None),
        P("sec", "mpo", None, None),
        P("sec", None),
        P("mpo"),
        P("sec", "mpo"),
    )
    return jax.shard_map(
        local, mesh=mesh, in_specs=placed, out_specs=P("sec", "mpo", None), check_vma=False
    )
```

```python
import functools

import jax
import jax.numpy as jnp
from jax import lax
from jax.experimental import pallas as pl
from jax.experimental.pallas import tpu as pltpu
from jax.sharding import PartitionSpec as P

AXES = ("sec", "mpo")
CUTS = (256, 256)
SHARES = ((3, 3), (4, 2), (2, 4))
FLIPS = {4: (3, 1, 2), 2: (1,), 1: ()}
VMEM = pl.BlockSpec(memory_space=pltpu.VMEM)
HBM = pl.BlockSpec(memory_space=pltpu.HBM)
PARAMS = pltpu.CompilerParams(vmem_limit_bytes=8 * 1024 * 1024)


def halo_pairs(sectors, group):
    pairs = []
    for sector in range(sectors):
        for place in range(group):
            there = sector + 1 if place % 2 == 0 else sector - 1
            if 0 <= there < sectors:
                pairs.append((sector * group + place, there * group + (place ^ 1)))
            elif group % 4 == 0:
                pairs.append((sector * group + place, sector * group + (place ^ 2)))
    return pairs


def group_pairs(sectors, group, flip):
    return [
        (sector * group + place, sector * group + (place ^ flip))
        for sector in range(sectors)
        for place in range(group)
    ]


def stages_of(group):
    bits, stages = (group // 2).bit_length() - 1, []
    while bits:
        taken = min(bits, 2)
        bits -= taken
        stages.append((bits, 1 << taken))
    return stages or [(0, 1)]


def parity(number):
    for shift in (8, 4, 2, 1):
        number = number ^ (number >> shift)
    return number & 1


def in_hbm(array):
    return pltpu.with_memory_space_constraint(array, pltpu.HBM)


def dot(a, b):
    return jnp.dot(a, b, preferred_element_type=jnp.float32)


def mask_kernel(start, dims_hbm, psi_hbm, out_ref, dims_ref, psi_ref, sems):
    parts = sems.shape[0] - 1
    rows, width = out_ref.shape[0] // parts, out_ref.shape[1]
    dims_copy = pltpu.make_async_copy(dims_hbm, dims_ref, sems.at[parts])
    dims_copy.start()
    copies = []
    for at in range(parts):
        from_ref = psi_hbm.at[0, pl.ds(at * rows, rows), pl.ds(start, width)]
        copies.append(pltpu.make_async_copy(from_ref, psi_ref.at[pl.ds(at * rows, rows)], sems.at[at]))
        copies[-1].start()
    dims_copy.wait()
    for at in range(parts):
        row = lax.broadcasted_iota(jnp.int32, (rows, width), 0) + at * rows
        col = lax.broadcasted_iota(jnp.int32, (rows, width), 1) + start
        keep = (row < dims_ref[0, 0] * 32) & (col < dims_ref[0, 1] * 32)
        copies[at].wait()
        piece = psi_ref[pl.ds(at * rows, rows)]
        out_ref[pl.ds(at * rows, rows)] = jnp.where(keep, piece, jnp.zeros_like(piece))


def mask(start, width, dims, psi):
    order, parts = psi.shape[1], 8
    return pl.pallas_call(
        functools.partial(mask_kernel, start),
        in_specs=[HBM, HBM],
        out_specs=VMEM,
        out_shape=pltpu.VMEM((order, width), psi.dtype),
        scratch_shapes=[
            pltpu.SMEM(dims.shape, jnp.int32),
            pltpu.VMEM((order, width), psi.dtype),
            pltpu.SemaphoreType.DMA((parts + 1,)),
        ],
        compiler_params=PARAMS,
        cost_estimate=pl.CostEstimate(flops=50000000000 if start else 0, bytes_accessed=0, transcendentals=0),
    )(in_hbm(dims), in_hbm(psi))


def load_kernel(sectors, dims_hbm, shift_hbm, connect_hbm, left_hbm, right_hbm, left_ref, right_ref, code_ref, keep_ref, dims_ref, shift_ref, connect_ref, sems):
    terms = left_ref.shape[0]
    scalars = [(dims_hbm, dims_ref), (shift_hbm, shift_ref), (connect_hbm, connect_ref)]
    copies = [pltpu.make_async_copy(a, b, sems.at[at]) for at, (a, b) in enumerate(scalars)]
    for term in range(terms):
        for which, (a, b) in enumerate(((left_hbm, left_ref), (right_hbm, right_ref))):
            copies.append(pltpu.make_async_copy(a.at[0, term], b.at[term], sems.at[len(copies)]))
    for copy in copies:
        copy.start()
    for copy in copies[:3]:
        copy.wait()

    sector, place = lax.axis_index("sec"), lax.axis_index("mpo")
    above = place % 2 == 0
    code = jnp.int32(0)
    for term in range(terms):
        shift = shift_ref[term]
        there = sector - shift
        used = (connect_ref[0, term] != 0) & (there >= 0) & (there < sectors)
        direct = (shift < 0) == above
        choice = jnp.where(shift == 0, 3, jnp.where(direct, 2, 1))
        code += jnp.where(used, choice, 0) << (2 * term)
    code_ref[...] = jnp.full(code_ref.shape, code, jnp.int32)

    rows = lax.broadcasted_iota(jnp.int32, keep_ref.shape, 0) + place * keep_ref.shape[0]
    cols = lax.broadcasted_iota(jnp.int32, keep_ref.shape, 1)
    keep = (rows < dims_ref[0, 0] * 32) & (cols < dims_ref[0, 1] * 32)
    keep_ref[...] = jnp.where(keep, 1.0, 0.0)
    for copy in copies[3:]:
        copy.wait()


def load(sectors, group, dims, term_shift, connect, left, right):
    _, terms, order, _ = left.shape
    return pl.pallas_call(
        functools.partial(load_kernel, sectors),
        in_specs=[HBM] * 5,
        out_specs=[VMEM] * 4,
        out_shape=[
            pltpu.VMEM(left.shape[1:], left.dtype),
            pltpu.VMEM(right.shape[1:], right.dtype),
            pltpu.VMEM((8, 128), jnp.int32),
            pltpu.VMEM((order // group, order), jnp.float32),
        ],
        scratch_shapes=[
            pltpu.SMEM(dims.shape, jnp.int32),
            pltpu.SMEM(term_shift.shape, jnp.int32),
            pltpu.SMEM(connect.shape, jnp.int32),
            pltpu.SemaphoreType.DMA((2 * terms + 3,)),
        ],
        compiler_params=PARAMS,
        cost_estimate=pl.CostEstimate(flops=4 * terms * order**3, bytes_accessed=4 * terms * order**2, transcendentals=0),
    )(*[in_hbm(array) for array in (dims, term_shift, connect, left, right)])


def row_blocks(group, height, flips):
    place = lax.axis_index("mpo")
    bit, ways = stages_of(group)[0]
    digit = (place >> (1 + bit)) & (ways - 1)
    firsts = []
    for flip in (0, *flips):
        for at in range(1 << bit):
            chip = ((digit ^ flip) << bit) + at
            firsts.append((2 * chip + (parity(place) ^ parity(chip))) * height)
    return [pl.ds(pl.multiple_of(first, height), height) for first in firsts]


def sources_first(code, terms):
    active, picks = jnp.int32(0), [jnp.int32(0)] * terms
    for wanted in (True, False):
        for term in range(terms):
            here = (((code >> (2 * term)) & 3) != 0) == wanted
            picks = [jnp.where(here & (active == at), term, pick) for at, pick in enumerate(picks)]
            active += jnp.where(here, 1, 0)
        if wanted:
            count = active
    return count, picks


def products(start, places, sources, groups, picked, first_ref):
    own, got, swapped = (ref[...] for ref in sources)
    width = own.shape[1]
    rights, column = [], 0
    for (code_ref, left_ref, right_ref, direct), picks in zip(groups, picked):
        code = code_ref[0, 0]
        for term in picks:
            choice = (code >> (2 * term)) & 3
            source = jnp.where(choice == direct, got, jnp.where(choice == 3 - direct, swapped, jnp.zeros_like(own)))
            source = jnp.where(choice == 3, own, source)
            left = left_ref[term] if places is None else jnp.concatenate([left_ref[term, at] for at in places], axis=0)
            first_ref[:, column : column + width] = dot(left, source).astype(jnp.bfloat16)
            column += width
            rights.append(right_ref[term, start : start + width])
    return dot(first_ref[:, :column], jnp.concatenate(rights, axis=0))


def sums_kernel(start, group, height, flips, last, *refs):
    sources, (code, left, right, code_2, left_2, right_2), refs = refs[:3], refs[3:9], refs[9:]
    terms, order, _ = left.shape
    groups = ((code, left, right, 2), (code_2, left_2.at[0], right_2.at[0], 1))
    places = row_blocks(group, height, flips)
    narrow = height % 16 == 0
    *before, first_ref, total_ref = refs[: -(2 + (1 + len(flips) if last else 1))] + refs[-2:]
    outs = refs[len(before) : -2]

    def run(picked):
        total = products(start, places if narrow else None, sources, groups, picked, first_ref)
        for ref in before:
            total += ref[...]
        if not last:
            outs[0][...] = total
            return
        if not narrow:
            total_ref[...] = total
        each = len(places) // len(outs)
        for which, out_ref in enumerate(outs):
            for at in range(each):
                block = which * each + at
                value = total[block * height : (block + 1) * height] if narrow else total_ref[places[block]]
                out_ref[at] = value.astype(out_ref.dtype)

    (count, picks), (count_2, picks_2) = (sources_first(ref[0, 0], terms) for ref in (code, code_2))
    taken = jnp.bool_(False)
    for few in SHARES:
        if terms != 4:
            break
        fits = (count <= few[0]) & (count_2 <= few[1])

        @pl.when(fits & jnp.logical_not(taken))
        def _():
            run((picks[: few[0]], picks_2[: few[1]]))

        taken = taken | fits

    @pl.when(jnp.logical_not(taken))
    def _():
        run((range(terms), range(terms)))


def sums(start, group, flips, last, sources, terms, before):
    count, order, _ = terms[1].shape
    height = order // group
    rows = order // 2 if height % 16 == 0 else order
    shape = (group // 2 // (1 + len(flips)), height, order)
    if last:
        outs = [pltpu.VMEM(shape, jnp.float32)] + [pltpu.VMEM(shape, jnp.bfloat16)] * len(flips)
    else:
        outs = [pltpu.VMEM((rows, order), jnp.float32)]
    operands = [*sources, *terms, *before]
    return pl.pallas_call(
        functools.partial(sums_kernel, start, group, height, flips, last),
        in_specs=[VMEM] * len(operands),
        out_specs=[VMEM] * len(outs),
        out_shape=outs,
        scratch_shapes=[
            pltpu.VMEM((rows, 2 * count * sources[0].shape[1]), jnp.bfloat16),
            pltpu.VMEM((order, order) if height % 16 else (8, 128), jnp.float32),
        ],
        compiler_params=PARAMS,
    )(*operands)


def split_kernel(bit, flips, *refs):
    ways = 1 + len(flips)
    *addends, own_ref = refs[: len(refs) - ways + 1]
    send_refs = refs[len(refs) - ways + 1 :]
    count = own_ref.shape[0]
    digit = (lax.axis_index("mpo") >> (1 + bit)) & (ways - 1)

    def summed(block):
        value = addends[0][block]
        for other in addends[1:]:
            value += other[block].astype(jnp.float32)
        return value

    for ref, flip in zip(send_refs, flips):
        for at in range(count):
            ref[at] = summed((digit ^ flip) * count + at).astype(ref.dtype)
    for at in range(count):
        own_ref[at] = summed(digit * count + at)


def split(addends, bit, flips):
    ways = 1 + len(flips)
    blocks, height, width = addends[0].shape
    shape = (blocks // ways, height, width)
    own, *sends = pl.pallas_call(
        functools.partial(split_kernel, bit, flips),
        in_specs=[VMEM] * len(addends),
        out_specs=[VMEM] * ways,
        out_shape=[pltpu.VMEM(shape, jnp.float32)] + [pltpu.VMEM(shape, jnp.bfloat16)] * (ways - 1),
        compiler_params=PARAMS,
    )(*addends)
    return sends, own


def local(psi, left_env, right_env, dims, term_shift, connect):
    sectors, group = lax.axis_size("sec"), lax.axis_size("mpo")
    order = psi.shape[1]

    pieces, start = [], 0
    for cut in CUTS:
        pieces.append(mask(start, cut, dims, psi))
        pieces[-1], psi = lax.optimization_barrier((pieces[-1], psi))
        start += cut
    to_core = group_pairs(sectors, group, 1)
    got = [lax.ppermute(piece, AXES, halo_pairs(sectors, group)) for piece in pieces]
    left_env, right_env, pieces[0] = lax.optimization_barrier((left_env, right_env, pieces[0]))
    left_2, right_2 = (lax.ppermute(env, AXES, to_core) for env in (left_env, right_env))
    left, right, code, keep = load(sectors, group, dims, term_shift, connect, left_env, right_env)
    code_2 = lax.ppermute(code, AXES, to_core)
    got[0], code = lax.optimization_barrier((got[0], code))
    got[-1], code_2 = lax.optimization_barrier((got[-1], code_2))
    swapped = [lax.ppermute(piece, AXES, to_core) for piece in got]

    terms = (code, left, right, code_2, left_2, right_2)
    stages = stages_of(group)
    start, addends = 0, []
    for at, cut in enumerate(CUTS):
        last = at == len(CUTS) - 1
        addends = sums(start, group, FLIPS[stages[0][1]], last, (pieces[at], got[at], swapped[at]), terms, addends)
        start += cut
    own, *sends = addends
    for at, (bit, ways) in enumerate(stages):
        if at > 0:
            sends, own = split(addends, bit, FLIPS[ways])
        addends = [own]
        for sent, flip in zip(sends, FLIPS[ways]):
            addends.append(lax.ppermute(sent, AXES, group_pairs(sectors, group, (flip << (1 + bit)) | parity(flip))))
    value = addends[0]
    for other in addends[1:]:
        value = value + other.astype(jnp.float32)
    value = jnp.where(keep != 0, value.reshape(keep.shape), 0.0)
    return value.astype(jnp.bfloat16)[None]


def solution(mesh):
    placed = (
        P("sec", None, None),
        P("sec", "mpo", None, None),
        P("sec", "mpo", None, None),
        P("sec", None),
        P("mpo"),
        P("sec", "mpo"),
    )
    return jax.shard_map(
        local, mesh=mesh, in_specs=placed, out_specs=P("sec", "mpo", None), check_vma=False
    )
```

```python
import functools

import jax
import jax.numpy as jnp
from jax import lax
from jax.experimental import pallas as pl
from jax.experimental.pallas import tpu as pltpu
from jax.sharding import PartitionSpec as P

AXES = ("sec", "mpo")
CUTS = (256, 256)
SHARES = {False: (), True: ((2, 4), (3, 3))}
FLIPS = {4: (3, 1, 2), 2: (1,), 1: ()}
VMEM = pl.BlockSpec(memory_space=pltpu.VMEM)
HBM = pl.BlockSpec(memory_space=pltpu.HBM)
PARAMS = pltpu.CompilerParams(vmem_limit_bytes=8 * 1024 * 1024)


def halo_pairs(sectors, group):
    pairs = []
    for sector in range(sectors):
        for place in range(group):
            there = sector + 1 if place % 2 == 0 else sector - 1
            if 0 <= there < sectors:
                pairs.append((sector * group + place, there * group + (place ^ 1)))
            elif group % 4 == 0:
                pairs.append((sector * group + place, sector * group + (place ^ 2)))
    return pairs


def group_pairs(sectors, group, flip):
    return [
        (sector * group + place, sector * group + (place ^ flip))
        for sector in range(sectors)
        for place in range(group)
    ]


def stages_of(group):
    bits, stages = (group // 2).bit_length() - 1, []
    while bits:
        taken = min(bits, 2)
        bits -= taken
        stages.append((bits, 1 << taken))
    return stages or [(0, 1)]


def parity(number):
    for shift in (8, 4, 2, 1):
        number = number ^ (number >> shift)
    return number & 1


def in_hbm(array):
    return pltpu.with_memory_space_constraint(array, pltpu.HBM)


def dot(a, b):
    return jnp.dot(a, b, preferred_element_type=jnp.float32)


def mask_kernel(start, dims_hbm, psi_hbm, out_ref, dims_ref, psi_ref, sems):
    parts = sems.shape[0] - 1
    rows, width = out_ref.shape[0] // parts, out_ref.shape[1]
    dims_copy = pltpu.make_async_copy(dims_hbm, dims_ref, sems.at[parts])
    dims_copy.start()
    copies = []
    for at in range(parts):
        from_ref = psi_hbm.at[0, pl.ds(at * rows, rows), pl.ds(start, width)]
        copies.append(pltpu.make_async_copy(from_ref, psi_ref.at[pl.ds(at * rows, rows)], sems.at[at]))
        copies[-1].start()
    dims_copy.wait()
    for at in range(parts):
        row = lax.broadcasted_iota(jnp.int32, (rows, width), 0) + at * rows
        col = lax.broadcasted_iota(jnp.int32, (rows, width), 1) + start
        keep = (row < dims_ref[0, 0] * 32) & (col < dims_ref[0, 1] * 32)
        copies[at].wait()
        piece = psi_ref[pl.ds(at * rows, rows)]
        out_ref[pl.ds(at * rows, rows)] = jnp.where(keep, piece, jnp.zeros_like(piece))


def mask(start, width, dims, psi):
    order, parts = psi.shape[1], 8
    return pl.pallas_call(
        functools.partial(mask_kernel, start),
        in_specs=[HBM, HBM],
        out_specs=VMEM,
        out_shape=pltpu.VMEM((order, width), psi.dtype),
        scratch_shapes=[
            pltpu.SMEM(dims.shape, jnp.int32),
            pltpu.VMEM((order, width), psi.dtype),
            pltpu.SemaphoreType.DMA((parts + 1,)),
        ],
        compiler_params=PARAMS,
        cost_estimate=pl.CostEstimate(flops=50000000000 if start else 0, bytes_accessed=0, transcendentals=0),
    )(in_hbm(dims), in_hbm(psi))


def load_kernel(sectors, dims_hbm, shift_hbm, connect_hbm, left_hbm, right_hbm, left_ref, right_ref, code_ref, keep_ref, dims_ref, shift_ref, connect_ref, sems):
    terms = left_ref.shape[0]
    scalars = [(dims_hbm, dims_ref), (shift_hbm, shift_ref), (connect_hbm, connect_ref)]
    copies = [pltpu.make_async_copy(a, b, sems.at[at]) for at, (a, b) in enumerate(scalars)]
    for term in range(terms):
        for which, (a, b) in enumerate(((left_hbm, left_ref), (right_hbm, right_ref))):
            copies.append(pltpu.make_async_copy(a.at[0, term], b.at[term], sems.at[len(copies)]))
    for copy in copies:
        copy.start()
    for copy in copies[:3]:
        copy.wait()

    sector, place = lax.axis_index("sec"), lax.axis_index("mpo")
    above = place % 2 == 0
    code = jnp.int32(0)
    for term in range(terms):
        shift = shift_ref[term]
        there = sector - shift
        used = (connect_ref[0, term] != 0) & (there >= 0) & (there < sectors)
        direct = (shift < 0) == above
        choice = jnp.where(shift == 0, 3, jnp.where(direct, 2, 1))
        code += jnp.where(used, choice, 0) << (2 * term)
    code_ref[...] = jnp.full(code_ref.shape, code, jnp.int32)

    rows = lax.broadcasted_iota(jnp.int32, keep_ref.shape, 0) + place * keep_ref.shape[0]
    cols = lax.broadcasted_iota(jnp.int32, keep_ref.shape, 1)
    keep = (rows < dims_ref[0, 0] * 32) & (cols < dims_ref[0, 1] * 32)
    keep_ref[...] = jnp.where(keep, 1.0, 0.0)
    for copy in copies[3:]:
        copy.wait()


def load(sectors, group, dims, term_shift, connect, left, right):
    _, terms, order, _ = left.shape
    return pl.pallas_call(
        functools.partial(load_kernel, sectors),
        in_specs=[HBM] * 5,
        out_specs=[VMEM] * 4,
        out_shape=[
            pltpu.VMEM(left.shape[1:], left.dtype),
            pltpu.VMEM(right.shape[1:], right.dtype),
            pltpu.VMEM((8, 128), jnp.int32),
            pltpu.VMEM((order // group, order), jnp.float32),
        ],
        scratch_shapes=[
            pltpu.SMEM(dims.shape, jnp.int32),
            pltpu.SMEM(term_shift.shape, jnp.int32),
            pltpu.SMEM(connect.shape, jnp.int32),
            pltpu.SemaphoreType.DMA((2 * terms + 3,)),
        ],
        compiler_params=PARAMS,
        cost_estimate=pl.CostEstimate(flops=4 * terms * order**3, bytes_accessed=4 * terms * order**2, transcendentals=0),
    )(*[in_hbm(array) for array in (dims, term_shift, connect, left, right)])


def row_blocks(group, height, flips):
    place = lax.axis_index("mpo")
    bit, ways = stages_of(group)[0]
    digit = (place >> (1 + bit)) & (ways - 1)
    firsts = []
    for flip in (0, *flips):
        for at in range(1 << bit):
            chip = ((digit ^ flip) << bit) + at
            firsts.append((2 * chip + (parity(place) ^ parity(chip))) * height)
    return [pl.ds(pl.multiple_of(first, height), height) for first in firsts]


def sources_first(code, terms):
    active, picks = jnp.int32(0), [jnp.int32(0)] * terms
    for wanted in (True, False):
        for term in range(terms):
            here = (((code >> (2 * term)) & 3) != 0) == wanted
            picks = [jnp.where(here & (active == at), term, pick) for at, pick in enumerate(picks)]
            active += jnp.where(here, 1, 0)
        if wanted:
            count = active
    return count, picks


def products(start, places, sources, groups, picked, first_ref):
    own, got, swapped = (ref[...] for ref in sources)
    width = own.shape[1]
    rights, column = [], 0
    for (code, left_ref, right_ref, direct), picks in zip(groups, picked):
        for term in picks:
            choice = (code >> (2 * term)) & 3
            source = jnp.where(choice == direct, got, jnp.where(choice == 3 - direct, swapped, jnp.zeros_like(own)))
            source = jnp.where(choice == 3, own, source)
            left = left_ref[term] if places is None else jnp.concatenate([left_ref[term, at] for at in places], axis=0)
            first_ref[:, column : column + width] = dot(left, source).astype(jnp.bfloat16)
            column += width
            rights.append(right_ref[term, start : start + width])
    return dot(first_ref[:, :column], jnp.concatenate(rights, axis=0))


def own_kernel(start, group, height, flips, own_ref, code_ref, left_ref, right_ref, total_ref, first_ref):
    places = row_blocks(group, height, flips)
    own, code = own_ref[...], code_ref[0, 0]
    terms, order, _ = left_ref.shape
    width = own.shape[1]
    for term in range(terms):
        source = jnp.where((code >> (2 * term)) & 3 == 3, own, jnp.zeros_like(own))
        left = left_ref[term] if height % 16 else jnp.concatenate([left_ref[term, at] for at in places], axis=0)
        first_ref[:, term * width : (term + 1) * width] = dot(left, source).astype(jnp.bfloat16)
    right = right_ref[:, start : start + width, :].reshape(terms * width, order)
    total_ref[...] = dot(first_ref[...], right)


def own_sums(start, group, flips, own, code, left, right):
    terms, order, _ = left.shape
    height = order // group
    rows = order // 2 if height % 16 == 0 else order
    return pl.pallas_call(
        functools.partial(own_kernel, start, group, height, flips),
        in_specs=[VMEM] * 4,
        out_specs=VMEM,
        out_shape=pltpu.VMEM((rows, order), jnp.float32),
        scratch_shapes=[pltpu.VMEM((rows, terms * own.shape[1]), jnp.bfloat16)],
        compiler_params=PARAMS,
    )(own, code, left, right)


def sums_kernel(start, group, height, flips, last, *refs):
    sources, (code, left, right, code_2, left_2, right_2), refs = refs[:3], refs[3:9], refs[9:]
    terms, order, _ = left.shape
    groups = ((code, left, right, 2), (code_2, left_2.at[0], right_2.at[0], 1))
    places = row_blocks(group, height, flips)
    narrow = height % 16 == 0
    *before, first_ref, total_ref = refs[: -(2 + (1 + len(flips) if last else 1))] + refs[-2:]
    outs = refs[len(before) : -2]

    def run(picked):
        total = products(start, places if narrow else None, sources, groups, picked, first_ref)
        for ref in before:
            total += ref[...]
        if not last:
            outs[0][...] = total
            return
        if not narrow:
            total_ref[...] = total
        each = len(places) // len(outs)
        for which, out_ref in enumerate(outs):
            for at in range(each):
                block = which * each + at
                value = total[block * height : (block + 1) * height] if narrow else total_ref[places[block]]
                out_ref[at] = value.astype(out_ref.dtype)

    numbers = [code[0, 0], code_2[0, 0]]
    if last:
        for term in range(terms):
            here = 3 << (2 * term)
            numbers[0] = jnp.where(numbers[0] & here == here, numbers[0] & ~here, numbers[0])
    groups = tuple((number, *rest) for number, (_, *rest) in zip(numbers, groups))
    (count, picks), (count_2, picks_2) = (sources_first(number, terms) for number in numbers)
    taken = jnp.bool_(False)
    for few in SHARES[last]:
        if terms != 4:
            break
        fits = (count <= few[0]) & (count_2 <= few[1])

        @pl.when(fits & jnp.logical_not(taken))
        def _():
            run((picks[: few[0]], picks_2[: few[1]]))

        taken = taken | fits

    @pl.when(jnp.logical_not(taken))
    def _():
        run((range(terms), range(terms)))


def sums(start, group, flips, last, sources, terms, before):
    count, order, _ = terms[1].shape
    height = order // group
    rows = order // 2 if height % 16 == 0 else order
    shape = (group // 2 // (1 + len(flips)), height, order)
    if last:
        outs = [pltpu.VMEM(shape, jnp.float32)] + [pltpu.VMEM(shape, jnp.bfloat16)] * len(flips)
    else:
        outs = [pltpu.VMEM((rows, order), jnp.float32)]
    operands = [*sources, *terms, *before]
    return pl.pallas_call(
        functools.partial(sums_kernel, start, group, height, flips, last),
        in_specs=[VMEM] * len(operands),
        out_specs=[VMEM] * len(outs),
        out_shape=outs,
        scratch_shapes=[
            pltpu.VMEM((rows, 2 * count * sources[0].shape[1]), jnp.bfloat16),
            pltpu.VMEM((order, order) if height % 16 else (8, 128), jnp.float32),
        ],
        compiler_params=PARAMS,
    )(*operands)


def split_kernel(bit, flips, *refs):
    ways = 1 + len(flips)
    *addends, own_ref = refs[: len(refs) - ways + 1]
    send_refs = refs[len(refs) - ways + 1 :]
    count = own_ref.shape[0]
    digit = (lax.axis_index("mpo") >> (1 + bit)) & (ways - 1)

    def summed(block):
        value = addends[0][block]
        for other in addends[1:]:
            value += other[block].astype(jnp.float32)
        return value

    for ref, flip in zip(send_refs, flips):
        for at in range(count):
            ref[at] = summed((digit ^ flip) * count + at).astype(ref.dtype)
    for at in range(count):
        own_ref[at] = summed(digit * count + at)


def split(addends, bit, flips):
    ways = 1 + len(flips)
    blocks, height, width = addends[0].shape
    shape = (blocks // ways, height, width)
    own, *sends = pl.pallas_call(
        functools.partial(split_kernel, bit, flips),
        in_specs=[VMEM] * len(addends),
        out_specs=[VMEM] * ways,
        out_shape=[pltpu.VMEM(shape, jnp.float32)] + [pltpu.VMEM(shape, jnp.bfloat16)] * (ways - 1),
        compiler_params=PARAMS,
    )(*addends)
    return sends, own


def local(psi, left_env, right_env, dims, term_shift, connect):
    sectors, group = lax.axis_size("sec"), lax.axis_size("mpo")
    order = psi.shape[1]

    pieces, start = [], 0
    for cut in CUTS:
        pieces.append(mask(start, cut, dims, psi))
        pieces[-1], psi = lax.optimization_barrier((pieces[-1], psi))
        start += cut
    to_core = group_pairs(sectors, group, 1)
    got = [lax.ppermute(piece, AXES, halo_pairs(sectors, group)) for piece in pieces]
    left_env, right_env, pieces[0] = lax.optimization_barrier((left_env, right_env, pieces[0]))
    left_2, right_2 = (lax.ppermute(env, AXES, to_core) for env in (left_env, right_env))
    left, right, code, keep = load(sectors, group, dims, term_shift, connect, left_env, right_env)
    code_2 = lax.ppermute(code, AXES, to_core)
    flips = FLIPS[stages_of(group)[0][1]]
    early = own_sums(sum(CUTS[:-1]), group, flips, pieces[-1], code, left, right)
    got[0], code, early = lax.optimization_barrier((got[0], code, early))
    got[-1], code_2 = lax.optimization_barrier((got[-1], code_2))
    swapped = [lax.ppermute(piece, AXES, to_core) for piece in got]

    terms = (code, left, right, code_2, left_2, right_2)
    stages = stages_of(group)
    start, addends = 0, [early]
    for at, cut in enumerate(CUTS):
        last = at == len(CUTS) - 1
        addends = sums(start, group, FLIPS[stages[0][1]], last, (pieces[at], got[at], swapped[at]), terms, addends)
        start += cut
    own, *sends = addends
    for at, (bit, ways) in enumerate(stages):
        if at > 0:
            sends, own = split(addends, bit, FLIPS[ways])
        addends = [own]
        for sent, flip in zip(sends, FLIPS[ways]):
            addends.append(lax.ppermute(sent, AXES, group_pairs(sectors, group, (flip << (1 + bit)) | parity(flip))))
    value = addends[0]
    for other in addends[1:]:
        value = value + other.astype(jnp.float32)
    value = jnp.where(keep != 0, value.reshape(keep.shape), 0.0)
    return value.astype(jnp.bfloat16)[None]


def solution(mesh):
    placed = (
        P("sec", None, None),
        P("sec", "mpo", None, None),
        P("sec", "mpo", None, None),
        P("sec", None),
        P("mpo"),
        P("sec", "mpo"),
    )
    return jax.shard_map(
        local, mesh=mesh, in_specs=placed, out_specs=P("sec", "mpo", None), check_vma=False
    )
```

```python
import functools

import jax
import jax.numpy as jnp
from jax import lax
from jax.experimental import pallas as pl
from jax.experimental.pallas import tpu as pltpu
from jax.sharding import PartitionSpec as P

AXES = ("sec", "mpo")
CUTS = (256, 256)
SHARES = {False: (), True: ((2, 3), (3, 3))}
FLIPS = {4: (3, 1, 2), 2: (1,), 1: ()}
VMEM = pl.BlockSpec(memory_space=pltpu.VMEM)
HBM = pl.BlockSpec(memory_space=pltpu.HBM)
PARAMS = pltpu.CompilerParams(vmem_limit_bytes=8 * 1024 * 1024)


def halo_pairs(sectors, group):
    pairs = []
    for sector in range(sectors):
        for place in range(group):
            there = sector + 1 if place % 2 == 0 else sector - 1
            if 0 <= there < sectors:
                pairs.append((sector * group + place, there * group + (place ^ 1)))
            elif group % 4 == 0:
                pairs.append((sector * group + place, sector * group + (place ^ 2)))
    return pairs


def group_pairs(sectors, group, flip):
    return [
        (sector * group + place, sector * group + (place ^ flip))
        for sector in range(sectors)
        for place in range(group)
    ]


def stages_of(group):
    bits, stages = (group // 2).bit_length() - 1, []
    while bits:
        taken = min(bits, 2)
        bits -= taken
        stages.append((bits, 1 << taken))
    return stages or [(0, 1)]


def parity(number):
    for shift in (8, 4, 2, 1):
        number = number ^ (number >> shift)
    return number & 1


def in_hbm(array):
    return pltpu.with_memory_space_constraint(array, pltpu.HBM)


def dot(a, b):
    return jnp.dot(a, b, preferred_element_type=jnp.float32)


def mask_kernel(start, dims_hbm, psi_hbm, out_ref, dims_ref, psi_ref, sems):
    parts = sems.shape[0] - 1
    rows, width = out_ref.shape[0] // parts, out_ref.shape[1]
    dims_copy = pltpu.make_async_copy(dims_hbm, dims_ref, sems.at[parts])
    dims_copy.start()
    copies = []
    for at in range(parts):
        from_ref = psi_hbm.at[0, pl.ds(at * rows, rows), pl.ds(start, width)]
        copies.append(pltpu.make_async_copy(from_ref, psi_ref.at[pl.ds(at * rows, rows)], sems.at[at]))
        copies[-1].start()
    dims_copy.wait()
    for at in range(parts):
        row = lax.broadcasted_iota(jnp.int32, (rows, width), 0) + at * rows
        col = lax.broadcasted_iota(jnp.int32, (rows, width), 1) + start
        keep = (row < dims_ref[0, 0] * 32) & (col < dims_ref[0, 1] * 32)
        copies[at].wait()
        piece = psi_ref[pl.ds(at * rows, rows)]
        out_ref[pl.ds(at * rows, rows)] = jnp.where(keep, piece, jnp.zeros_like(piece))


def mask(start, width, dims, psi):
    order, parts = psi.shape[1], 8
    return pl.pallas_call(
        functools.partial(mask_kernel, start),
        in_specs=[HBM, HBM],
        out_specs=VMEM,
        out_shape=pltpu.VMEM((order, width), psi.dtype),
        scratch_shapes=[
            pltpu.SMEM(dims.shape, jnp.int32),
            pltpu.VMEM((order, width), psi.dtype),
            pltpu.SemaphoreType.DMA((parts + 1,)),
        ],
        compiler_params=PARAMS,
        cost_estimate=pl.CostEstimate(flops=50000000000 if start else 0, bytes_accessed=0, transcendentals=0),
    )(in_hbm(dims), in_hbm(psi))


def load_kernel(sectors, dims_hbm, shift_hbm, connect_hbm, left_hbm, right_hbm, left_ref, right_ref, code_ref, keep_ref, dims_ref, shift_ref, connect_ref, sems):
    terms = left_ref.shape[0]
    scalars = [(dims_hbm, dims_ref), (shift_hbm, shift_ref), (connect_hbm, connect_ref)]
    copies = [pltpu.make_async_copy(a, b, sems.at[at]) for at, (a, b) in enumerate(scalars)]
    for term in range(terms):
        for which, (a, b) in enumerate(((left_hbm, left_ref), (right_hbm, right_ref))):
            copies.append(pltpu.make_async_copy(a.at[0, term], b.at[term], sems.at[len(copies)]))
    for copy in copies:
        copy.start()
    for copy in copies[:3]:
        copy.wait()

    sector, place = lax.axis_index("sec"), lax.axis_index("mpo")
    above = place % 2 == 0
    code = jnp.int32(0)
    for term in range(terms):
        shift = shift_ref[term]
        there = sector - shift
        used = (connect_ref[0, term] != 0) & (there >= 0) & (there < sectors)
        direct = (shift < 0) == above
        choice = jnp.where(shift == 0, 3, jnp.where(direct, 2, 1))
        code += jnp.where(used, choice, 0) << (2 * term)
    code_ref[...] = jnp.full(code_ref.shape, code, jnp.int32)

    rows = lax.broadcasted_iota(jnp.int32, keep_ref.shape, 0) + place * keep_ref.shape[0]
    cols = lax.broadcasted_iota(jnp.int32, keep_ref.shape, 1)
    keep = (rows < dims_ref[0, 0] * 32) & (cols < dims_ref[0, 1] * 32)
    keep_ref[...] = jnp.where(keep, 1.0, 0.0)
    for copy in copies[3:]:
        copy.wait()


def load(sectors, group, dims, term_shift, connect, left, right):
    _, terms, order, _ = left.shape
    return pl.pallas_call(
        functools.partial(load_kernel, sectors),
        in_specs=[HBM] * 5,
        out_specs=[VMEM] * 4,
        out_shape=[
            pltpu.VMEM(left.shape[1:], left.dtype),
            pltpu.VMEM(right.shape[1:], right.dtype),
            pltpu.VMEM((8, 128), jnp.int32),
            pltpu.VMEM((order // group, order), jnp.float32),
        ],
        scratch_shapes=[
            pltpu.SMEM(dims.shape, jnp.int32),
            pltpu.SMEM(term_shift.shape, jnp.int32),
            pltpu.SMEM(connect.shape, jnp.int32),
            pltpu.SemaphoreType.DMA((2 * terms + 3,)),
        ],
        compiler_params=PARAMS,
        cost_estimate=pl.CostEstimate(flops=4 * terms * order**3, bytes_accessed=4 * terms * order**2, transcendentals=0),
    )(*[in_hbm(array) for array in (dims, term_shift, connect, left, right)])


def row_blocks(group, height, flips):
    place = lax.axis_index("mpo")
    bit, ways = stages_of(group)[0]
    digit = (place >> (1 + bit)) & (ways - 1)
    firsts = []
    for flip in (0, *flips):
        for at in range(1 << bit):
            chip = ((digit ^ flip) << bit) + at
            firsts.append((2 * chip + (parity(place) ^ parity(chip))) * height)
    return [pl.ds(pl.multiple_of(first, height), height) for first in firsts]


def sources_first(code, terms):
    active, picks = jnp.int32(0), [jnp.int32(0)] * terms
    for wanted in (True, False):
        for term in range(terms):
            here = (((code >> (2 * term)) & 3) != 0) == wanted
            picks = [jnp.where(here & (active == at), term, pick) for at, pick in enumerate(picks)]
            active += jnp.where(here, 1, 0)
        if wanted:
            count = active
    return count, picks


def products(start, places, sources, groups, picked, first_ref):
    own, got, swapped = (ref[...] for ref in sources)
    width = own.shape[1]
    rights, column = [], 0
    for (code, left_ref, right_ref, direct), picks in zip(groups, picked):
        for term in picks:
            choice = (code >> (2 * term)) & 3
            source = jnp.where(choice == direct, got, jnp.where(choice == 3 - direct, swapped, jnp.zeros_like(own)))
            source = jnp.where(choice == 3, own, source)
            left = left_ref[term] if places is None else jnp.concatenate([left_ref[term, at] for at in places], axis=0)
            first_ref[:, column : column + width] = dot(left, source).astype(jnp.bfloat16)
            column += width
            rights.append(right_ref[term, start : start + width])
    return dot(first_ref[:, :column], jnp.concatenate(rights, axis=0))


def own_kernel(start, group, height, flips, own_ref, code_ref, left_ref, right_ref, total_ref, first_ref):
    places = row_blocks(group, height, flips)
    own, code = own_ref[...], code_ref[0, 0]
    terms, order, _ = left_ref.shape
    width = own.shape[1]
    for term in range(terms):
        source = jnp.where((code >> (2 * term)) & 3 == 3, own, jnp.zeros_like(own))
        left = left_ref[term] if height % 16 else jnp.concatenate([left_ref[term, at] for at in places], axis=0)
        first_ref[:, term * width : (term + 1) * width] = dot(left, source).astype(jnp.bfloat16)
    right = right_ref[:, start : start + width, :].reshape(terms * width, order)
    total_ref[...] = dot(first_ref[...], right)


def own_sums(start, group, flips, own, code, left, right):
    terms, order, _ = left.shape
    height = order // group
    rows = order // 2 if height % 16 == 0 else order
    return pl.pallas_call(
        functools.partial(own_kernel, start, group, height, flips),
        in_specs=[VMEM] * 4,
        out_specs=VMEM,
        out_shape=pltpu.VMEM((rows, order), jnp.float32),
        scratch_shapes=[pltpu.VMEM((rows, terms * own.shape[1]), jnp.bfloat16)],
        compiler_params=PARAMS,
    )(own, code, left, right)


def sums_kernel(start, group, height, flips, last, *refs):
    sources, (code, left, right, code_2, left_2, right_2), refs = refs[:3], refs[3:9], refs[9:]
    terms, order, _ = left.shape
    groups = ((code, left, right, 2), (code_2, left_2.at[0], right_2.at[0], 1))
    places = row_blocks(group, height, flips)
    narrow = height % 16 == 0
    *before, first_ref, total_ref = refs[: -(2 + (1 + len(flips) if last else 1))] + refs[-2:]
    outs = refs[len(before) : -2]

    def run(picked):
        total = products(start, places if narrow else None, sources, groups, picked, first_ref)
        for ref in before:
            total += ref[...]
        if not last:
            outs[0][...] = total
            return
        if not narrow:
            total_ref[...] = total
        each = len(places) // len(outs)
        for which, out_ref in enumerate(outs):
            for at in range(each):
                block = which * each + at
                value = total[block * height : (block + 1) * height] if narrow else total_ref[places[block]]
                out_ref[at] = value.astype(out_ref.dtype)

    numbers = [code[0, 0], code_2[0, 0]]
    if last:
        for term in range(terms):
            here = 3 << (2 * term)
            numbers[0] = jnp.where(numbers[0] & here == here, numbers[0] & ~here, numbers[0])
    groups = tuple((number, *rest) for number, (_, *rest) in zip(numbers, groups))
    (count, picks), (count_2, picks_2) = (sources_first(number, terms) for number in numbers)
    taken = jnp.bool_(False)
    for few in SHARES[last]:
        if terms != 4:
            break
        fits = (count <= few[0]) & (count_2 <= few[1])

        @pl.when(fits & jnp.logical_not(taken))
        def _():
            run((picks[: few[0]], picks_2[: few[1]]))

        taken = taken | fits

    @pl.when(jnp.logical_not(taken))
    def _():
        run((range(terms), range(terms)))


def sums(start, group, flips, last, sources, terms, before):
    count, order, _ = terms[1].shape
    height = order // group
    rows = order // 2 if height % 16 == 0 else order
    shape = (group // 2 // (1 + len(flips)), height, order)
    if last:
        outs = [pltpu.VMEM(shape, jnp.float32)] + [pltpu.VMEM(shape, jnp.bfloat16)] * len(flips)
    else:
        outs = [pltpu.VMEM((rows, order), jnp.float32)]
    operands = [*sources, *terms, *before]
    return pl.pallas_call(
        functools.partial(sums_kernel, start, group, height, flips, last),
        in_specs=[VMEM] * len(operands),
        out_specs=[VMEM] * len(outs),
        out_shape=outs,
        scratch_shapes=[
            pltpu.VMEM((rows, 2 * count * sources[0].shape[1]), jnp.bfloat16),
            pltpu.VMEM((order, order) if height % 16 else (8, 128), jnp.float32),
        ],
        compiler_params=PARAMS,
    )(*operands)


def split_kernel(bit, flips, *refs):
    ways = 1 + len(flips)
    *addends, own_ref = refs[: len(refs) - ways + 1]
    send_refs = refs[len(refs) - ways + 1 :]
    count = own_ref.shape[0]
    digit = (lax.axis_index("mpo") >> (1 + bit)) & (ways - 1)

    def summed(block):
        value = addends[0][block]
        for other in addends[1:]:
            value += other[block].astype(jnp.float32)
        return value

    for ref, flip in zip(send_refs, flips):
        for at in range(count):
            ref[at] = summed((digit ^ flip) * count + at).astype(ref.dtype)
    for at in range(count):
        own_ref[at] = summed(digit * count + at)


def split(addends, bit, flips):
    ways = 1 + len(flips)
    blocks, height, width = addends[0].shape
    shape = (blocks // ways, height, width)
    own, *sends = pl.pallas_call(
        functools.partial(split_kernel, bit, flips),
        in_specs=[VMEM] * len(addends),
        out_specs=[VMEM] * ways,
        out_shape=[pltpu.VMEM(shape, jnp.float32)] + [pltpu.VMEM(shape, jnp.bfloat16)] * (ways - 1),
        compiler_params=PARAMS,
    )(*addends)
    return sends, own


def local(psi, left_env, right_env, dims, term_shift, connect):
    sectors, group = lax.axis_size("sec"), lax.axis_size("mpo")
    order = psi.shape[1]

    pieces, start = [], 0
    for cut in CUTS:
        pieces.append(mask(start, cut, dims, psi))
        pieces[-1], psi = lax.optimization_barrier((pieces[-1], psi))
        start += cut
    to_core = group_pairs(sectors, group, 1)
    got = [lax.ppermute(piece, AXES, halo_pairs(sectors, group)) for piece in pieces]
    left_env, right_env, pieces[0] = lax.optimization_barrier((left_env, right_env, pieces[0]))
    left_2, right_2 = (lax.ppermute(env, AXES, to_core) for env in (left_env, right_env))
    left, right, code, keep = load(sectors, group, dims, term_shift, connect, left_env, right_env)
    code_2 = lax.ppermute(code, AXES, to_core)
    flips = FLIPS[stages_of(group)[0][1]]
    early = own_sums(sum(CUTS[:-1]), group, flips, pieces[-1], code, left, right)
    got[0], code, early = lax.optimization_barrier((got[0], code, early))
    got[-1], code_2 = lax.optimization_barrier((got[-1], code_2))
    swapped = [lax.ppermute(piece, AXES, to_core) for piece in got]

    terms = (code, left, right, code_2, left_2, right_2)
    stages = stages_of(group)
    start, addends = 0, [early]
    for at, cut in enumerate(CUTS):
        last = at == len(CUTS) - 1
        addends = sums(start, group, FLIPS[stages[0][1]], last, (pieces[at], got[at], swapped[at]), terms, addends)
        start += cut
    own, *sends = addends
    for at, (bit, ways) in enumerate(stages):
        if at > 0:
            sends, own = split(addends, bit, FLIPS[ways])
        addends = [own]
        for sent, flip in zip(sends, FLIPS[ways]):
            addends.append(lax.ppermute(sent, AXES, group_pairs(sectors, group, (flip << (1 + bit)) | parity(flip))))
    value = addends[0]
    for other in addends[1:]:
        value = value + other.astype(jnp.float32)
    value = jnp.where(keep != 0, value.reshape(keep.shape), 0.0)
    return value.astype(jnp.bfloat16)[None]


def solution(mesh):
    placed = (
        P("sec", None, None),
        P("sec", "mpo", None, None),
        P("sec", "mpo", None, None),
        P("sec", None),
        P("mpo"),
        P("sec", "mpo"),
    )
    return jax.shard_map(
        local, mesh=mesh, in_specs=placed, out_specs=P("sec", "mpo", None), check_vma=False
    )
```
